32 devices in a mesh: dp: 8 (over y, x, core), seq: 4 (over z).
Axes of the slice: x: 2, y: 2, z: 4, core: 2. Of those that a mesh axis runs over, the one named last changes fastest.
Arguments:
- inputs: bfloat16 [8, 1024, 2048], P('dp', 'seq'), may hold values from -6 to 6
- lengths: int32 [8], P('dp'), may hold values from 769 to 1024, as said below
- positions: int32 [8, 1024], P('dp', 'seq'), may hold values from 0 to 4093, as said below
- attn_gain: bfloat16 [2048], P(('dp', 'seq')), may hold values from 0.5 to 1.5
- w_query: bfloat16 [2048, 2048], P(('dp', 'seq')), may hold values from -0.125 to 0.125
- w_key: bfloat16 [2048, 512], P(('dp', 'seq')), may hold values from -0.125 to 0.125
- w_value: bfloat16 [2048, 512], P(('dp', 'seq')), may hold values from -0.125 to 0.125
- w_output: bfloat16 [2048, 2048], P(('dp', 'seq')), may hold values from -3 to 3
- ffn_gain: bfloat16 [2048], P(('dp', 'seq')), may hold values from 0.5 to 1.5
- w_gate: bfloat16 [2048, 8192], P(('dp', 'seq')), may hold values from -0.125 to 0.125
- w_up: bfloat16 [2048, 8192], P(('dp', 'seq')), may hold values from -0.125 to 0.125
- w_down: bfloat16 [2048, 8192], P(('dp', 'seq')), may hold values from -0.0625 to 0.0625
- out_grad: bfloat16 [8, 1024, 2048], P('dp', 'seq'), may hold values from -6 to 6
Outputs:
- output: bfloat16 [8, 1024, 2048], P('dp', 'seq')
- input_grad: bfloat16 [8, 1024, 2048], P('dp', 'seq')
- attn_gain_grad: float32 [2048], P(('dp', 'seq'))
- w_query_grad: float32 [2048, 2048], P(('dp', 'seq'))
- w_key_grad: float32 [2048, 512], P(('dp', 'seq'))
- w_value_grad: float32 [2048, 512], P(('dp', 'seq'))
- w_output_grad: float32 [2048, 2048], P(('dp', 'seq'))
- ffn_gain_grad: float32 [2048], P(('dp', 'seq'))
- w_gate_grad: float32 [2048, 8192], P(('dp', 'seq'))
- w_up_grad: float32 [2048, 8192], P(('dp', 'seq'))
- w_down_grad: float32 [2048, 8192], P(('dp', 'seq'))
The draws below stay inside these ranges and needn't reach their ends.
Inputs may be any that keep to these rules, and one draw needn't show every extreme that they name: Each sequence's valid tokens are the first lengths slots; in every draw at least one sequence fills all 1024 slots. Within a sequence, positions rise by 1 or 2 from each slot to the next; a sequence's first position lies from 0 to 2047; in every draw some sequence starts at 0, and another starts at 2047 and rises by 2 at every slot.
All inputs are finite; a program needn't handle non-finite values.
Results may differ from the reference program's by a relative error of at most 0.014.
Values may be sent and summed in bfloat16 or wider, within the bound.
A program may use at most 704 MiB of HBM per device.

```python
import math
import jax
import jax.numpy as jnp
from jax import lax

D = 2048
QUERY_HEADS = 32
KEY_VALUE_HEADS = 8
HEAD_SIZE = 64
FF = 8192
SEQUENCE_SLOTS = 1024
QW = 2048
KW = 512
SEQS = 8


def draw_lengths(key, part):
    drawn = jax.random.randint(jax.random.fold_in(key, 11), (SEQS,), SEQUENCE_SLOTS - SEQUENCE_SLOTS // 4 + 1, SEQUENCE_SLOTS + 1)
    chosen = jax.random.randint(jax.random.fold_in(key, 12), (), 0, SEQS)
    return jnp.where(jnp.arange(SEQS) == chosen, SEQUENCE_SLOTS, drawn).astype(jnp.int32)


def draw_positions(key, part):
    starts = jax.random.randint(jax.random.fold_in(key, 21), (SEQS,), 0, 2048)
    chosen = jax.random.randint(jax.random.fold_in(key, 22), (), 0, SEQS)
    other = (chosen + 1 + jax.random.randint(jax.random.fold_in(key, 23), (), 0, SEQS - 1)) % SEQS
    order = jnp.arange(SEQS)
    starts = jnp.where(order == chosen, 0, jnp.where(order == other, 2047, starts))
    strides = jax.random.randint(jax.random.fold_in(key, 24), (SEQS, SEQUENCE_SLOTS - 1), 1, 3)
    strides = jnp.where((order == other)[:, None], 2, strides)
    steps_taken = jnp.concatenate([jnp.zeros((SEQS, 1), jnp.int32), jnp.cumsum(strides, axis=1).astype(jnp.int32)], axis=1)
    return (starts[:, None] + steps_taken).astype(jnp.int32)


def spiked(values, rng, source, target, parts, factor):
    def block_of(position):
        return (jnp.arange(values.shape[position]) // (values.shape[position] // parts)).reshape((-1,) + (1,) * (values.ndim - 1 - position))

    first = jax.random.permutation(rng, parts)[block_of(target)]
    other_side = (block_of(target) + parts // 2) % parts
    return jnp.where((block_of(source) == first) | (block_of(source) == other_side), factor * values, values)


def block_levels(stream_key, shape, pieces, low, top_value):
    loudness = 1.0
    for position, blocks in pieces:
        steps = jax.random.uniform(jax.random.fold_in(jax.random.fold_in(stream_key, 6), position), (blocks,), jnp.float32, low / len(pieces), top_value / len(pieces))
        loudness = loudness * jnp.repeat(jnp.exp(steps), shape[position] // blocks).reshape((-1,) + (1,) * (len(shape) - 1 - position))
    return loudness


def noise(own_key, dims, deviation, reach, cuts=(), kind=jnp.bfloat16):
    values = deviation * jax.random.normal(own_key, dims, jnp.float32)
    if cuts:
        values = values * block_levels(own_key, dims, cuts, -0.22, 0.18)
    return jnp.clip(values, -reach, reach).astype(kind)


def bell_draw_with(own_key, shape, scale, most, pieces, heavy, kind=jnp.bfloat16):
    array = scale * jax.random.normal(own_key, shape, jnp.float32)
    if pieces:
        array = array * block_levels(own_key, shape, pieces, -0.22, 0.18)
    return jnp.clip(spiked(array, jax.random.fold_in(own_key, 3), *heavy), -most, most).astype(kind)


def setup_inputs(seed: int = 0) -> dict:
    streams_of = jax.random.split(jax.random.key(seed), 14)
    return {
        "inputs": bell_draw_with(streams_of[0], (SEQS, SEQUENCE_SLOTS, D), 1.0, 6.0, ((0, 8), (1, 4)), (0, 2, 8, 2.0)),
        "lengths": draw_lengths(jax.random.fold_in(streams_of[13], 71), 0),
        "positions": draw_positions(jax.random.fold_in(streams_of[13], 71), 0),
        "attn_gain": jnp.clip(1.0 + 0.1 * jax.random.normal(streams_of[3], (D,), jnp.float32), 0.5, 1.5).astype(jnp.bfloat16),
        "w_query": noise(streams_of[4], (D, QW), D ** -0.5, 0.125, ((0, 32),)),
        "w_key": noise(streams_of[5], (D, KW), D ** -0.5, 0.125, ((0, 32),)),
        "w_value": noise(streams_of[6], (D, KW), D ** -0.5, 0.125, ((0, 32),)),
        "w_output": noise(streams_of[7], (QW, D), (max(1, QW // (SEQUENCE_SLOTS // 2))) ** -0.5, 3.0, ((0, 32),)),
        "ffn_gain": jnp.clip(1.0 + 0.1 * jax.random.normal(streams_of[8], (D,), jnp.float32), 0.5, 1.5).astype(jnp.bfloat16),
        "w_gate": noise(streams_of[9], (D, FF), D ** -0.5, 0.125, ((0, 32),)),
        "w_up": noise(streams_of[10], (D, FF), D ** -0.5, 0.125, ((0, 32),)),
        "w_down": noise(streams_of[11], (D, FF), FF ** -0.5, 0.0625, ((0, 32),)),
        "out_grad": noise(streams_of[12], (SEQS, SEQUENCE_SLOTS, D), 1.0, 6.0, ((0, 8), (1, 4))),
    }


epsilon = 1e-05
rope_base = 500000.0
scale_factor = 32.0
high_factor = 4.0
initial_context = 8192.0
masked_score = -1e+30
highest_precision = lax.Precision.HIGHEST

@jax.custom_vjp
def lower_precision(v):
    return lax.optimization_barrier(v.astype(jnp.bfloat16)).astype(jnp.float32)

@jax.custom_vjp
def low_back(v):
    return v

def low_keep(v):
    return (lower_precision(v), None)

def low_pass(kept, grad):
    return (grad,)

def back_keep(v):
    return (v, None)

def back_low(kept, grad):
    return (lower_precision(grad),)
lower_precision.defvjp(low_keep, low_pass)
low_back.defvjp(back_keep, back_low)

def rope_tables(positions):
    halves_index = jnp.arange(HEAD_SIZE // 2, dtype=jnp.float32)
    frequency = 1.0 / rope_base ** (2.0 * halves_index / HEAD_SIZE)
    wavelength = 2.0 * math.pi / frequency
    blending = (initial_context / wavelength - 1.0) / (high_factor - 1.0)
    middle = (1.0 - blending) * frequency / scale_factor + blending * frequency
    scaled = jnp.where(wavelength < initial_context / high_factor, frequency, jnp.where(wavelength > initial_context, frequency / scale_factor, middle))
    angles = positions.astype(jnp.float32)[..., None] * scaled
    angles = jnp.concatenate([angles, angles], axis=-1)
    return (jnp.cos(angles), jnp.sin(angles))

def apply_rotary(vector, cos_table, sin_table):
    first_half, second_half = jnp.split(vector, 2, axis=-1)
    return vector * cos_table + jnp.concatenate([-second_half, first_half], axis=-1) * sin_table

def rms_norm(values, scaling):
    return values * lax.rsqrt(lax.optimization_barrier(jnp.mean(values * values, axis=-1, keepdims=True)) + epsilon) * scaling

def block_forward(tokens, attn_gain, w_query, w_key, w_value, w_output, ffn_gain, w_gate, w_up, w_down, cos_table, sin_table, length):
    slot_ids = jnp.arange(SEQUENCE_SLOTS, dtype=jnp.int32)
    valid = (slot_ids < length)[:, None]
    allowed = (slot_ids[None, :] <= slot_ids[:, None]) & (slot_ids[None, :] < length)
    normed_attn = lower_precision(rms_norm(tokens, attn_gain))
    query_pre = low_back(jnp.dot(normed_attn, w_query, precision=highest_precision))
    key_projected = low_back(jnp.dot(normed_attn, w_key, precision=highest_precision))
    value_lower = lower_precision(low_back(jnp.dot(normed_attn, w_value, precision=highest_precision)))
    cosine_heads = cos_table[:, None, :]
    sine_heads = sin_table[:, None, :]
    query_rotated = lower_precision(apply_rotary(query_pre.reshape(SEQUENCE_SLOTS, QUERY_HEADS, HEAD_SIZE), cosine_heads, sine_heads))
    key_rotated = lower_precision(apply_rotary(key_projected.reshape(SEQUENCE_SLOTS, KEY_VALUE_HEADS, HEAD_SIZE), cosine_heads, sine_heads))
    grouped_queries = query_rotated.reshape(SEQUENCE_SLOTS, KEY_VALUE_HEADS, QUERY_HEADS // KEY_VALUE_HEADS, HEAD_SIZE)
    raw_scores = jnp.einsum('qhgd,khd->hgqk', grouped_queries, key_rotated, precision=highest_precision) * HEAD_SIZE ** (-0.5)
    scores = low_back(jnp.where(allowed, raw_scores, masked_score))
    row_peak = lax.optimization_barrier(jnp.max(scores, axis=-1, keepdims=True))
    exponent = jnp.exp(scores - row_peak)
    attention_probabilities = lower_precision(exponent / lax.optimization_barrier(jnp.sum(exponent, axis=-1, keepdims=True)))
    attended_rows = jnp.einsum('xnif,fxu->ixnu', attention_probabilities, value_lower.reshape(SEQUENCE_SLOTS, KEY_VALUE_HEADS, HEAD_SIZE), precision=highest_precision).reshape(SEQUENCE_SLOTS, QUERY_HEADS * HEAD_SIZE)
    attended_rows = lower_precision(low_back(attended_rows))
    hidden_res = tokens + low_back(jnp.dot(attended_rows, w_output, precision=highest_precision))
    normed_ffn = lower_precision(rms_norm(hidden_res, ffn_gain))
    gate_pre = low_back(jnp.dot(normed_ffn, w_gate, precision=highest_precision))
    upward = low_back(jnp.dot(normed_ffn, w_up, precision=highest_precision))
    activated = lower_precision(jax.nn.silu(gate_pre) * upward)
    result = hidden_res + low_back(jnp.dot(activated, w_down.T, precision=highest_precision))
    return jnp.where(valid, result, 0.0)

def reference(inputs, lengths, positions, attn_gain, w_query, w_key, w_value, w_output, ffn_gain, w_gate, w_up, w_down, out_grad):
    weights = tuple((weight.astype(jnp.float32) for weight in (attn_gain, w_query, w_key, w_value, w_output, ffn_gain, w_gate, w_up, w_down)))
    cos_table, sin_table = rope_tables(positions)

    def per_sequence(totals, sequence_items):
        seq_tokens, seq_length, seq_cos, seq_sin, seq_cotangent = sequence_items

        def forward(tokens_f, *params):
            return block_forward(tokens_f, *params, seq_cos, seq_sin, seq_length)
        result, pullback = jax.vjp(forward, seq_tokens.astype(jnp.float32), *weights)
        gradients = pullback(seq_cotangent.astype(jnp.float32))
        new_totals = jax.tree.map(jnp.add, totals, tuple(gradients[1:]))
        return (new_totals, (result.astype(jnp.bfloat16), gradients[0].astype(jnp.bfloat16)))
    starting = tuple((jnp.zeros(weight.shape, jnp.float32) for weight in weights))
    totals, (outputs, input_grads) = lax.scan(per_sequence, starting, (inputs, lengths, cos_table, sin_table, out_grad))
    return (outputs, input_grads, totals[0], totals[1], totals[2], totals[3], totals[4], totals[5], totals[6], totals[7], totals[8])
```

```python
import functools
import math

import jax
import jax.numpy as jnp
from jax import lax
from jax.experimental import pallas as pl
from jax.experimental.pallas import tpu as pltpu
from jax.sharding import Mesh
from jax.sharding import PartitionSpec as P

HEADS = 32
GROUPS = 8
SIZE = 64
SHARE = HEADS // GROUPS
EPS = 1e-05
TEAM = ("b", "c", "l")
EVERY = ("a", "b", "c", "h", "l")
BF = jnp.bfloat16
F32 = jnp.float32


def rope_tables(positions):
    index = jnp.arange(SIZE // 2, dtype=F32)
    frequency = 1.0 / 500000.0 ** (2.0 * index / SIZE)
    wavelength = 2.0 * math.pi / frequency
    blending = (8192.0 / wavelength - 1.0) / (4.0 - 1.0)
    middle = (1.0 - blending) * frequency / 32.0 + blending * frequency
    scaled = jnp.where(
        wavelength < 8192.0 / 4.0,
        frequency,
        jnp.where(wavelength > 8192.0, frequency / 32.0, middle),
    )
    angles = positions.astype(F32)[..., None] * scaled
    angles = jnp.concatenate([angles, angles], axis=-1)
    return jnp.cos(angles), jnp.sin(angles)


def rotate(v, cosine, sine):
    first, second = jnp.split(v, 2, axis=-1)
    return v * cosine + jnp.concatenate([-second, first], axis=-1) * sine


def rotate_back(v, cosine, sine):
    turned = v * sine
    first, second = jnp.split(turned, 2, axis=-1)
    return v * cosine + jnp.concatenate([second, -first], axis=-1)


def shift(value, axis, step):
    n = lax.axis_size(axis)
    return lax.ppermute(value, axis, [(i, (i + step) % n) for i in range(n)])


def scatter_step(value, axis, dim):
    n = lax.axis_size(axis)
    me = lax.axis_index(axis)
    kept = lax.dynamic_index_in_dim(value, me, dim, keepdims=False)
    for s in range(1, n):
        sent = lax.dynamic_index_in_dim(value, lax.rem(me + s, n), dim, keepdims=False)
        kept = kept + shift(sent.astype(BF), axis, s).astype(F32)
    return kept


def team_scatter(partial):
    width = partial.shape[-1]
    view = partial.reshape(2, 2, 2, -1, width)
    view = scatter_step(view, "c", 1)
    left = scatter_step(view[..., : width // 2], "l", 1)
    left = scatter_step(left, "b", 0)
    right = scatter_step(view[..., width // 2 :], "b", 0)
    right = scatter_step(right, "l", 0)
    return jnp.concatenate([left, right], axis=-1)


def slices_of(weight, rows):
    return weight.reshape(rows, 8, -1)


def gather_slices(local):
    rows, _, width = local.shape
    n_a, n_h = lax.axis_size("a"), lax.axis_size("h")
    a, h = lax.axis_index("a"), lax.axis_index("h")
    piece = lax.all_to_all(local.transpose(1, 0, 2), TEAM, 0, 0, tiled=True)
    whole = jnp.zeros((n_a, 4, n_h, 2 * rows, width), local.dtype)
    for dh in range(n_h):
        from_h = shift(piece, "h", -dh) if dh else piece
        for da in range(n_a):
            block = shift(from_h, "a", -da) if da else from_h
            whole = lax.dynamic_update_slice(
                whole,
                block.reshape(1, 4, 1, 2 * rows, width),
                (lax.rem(a + da, n_a), 0, lax.rem(h + dh, n_h), 0, 0),
            )
    return whole.reshape(-1, width)


def scatter_slices(partial, rows):
    width = partial.shape[-1]
    view = partial.reshape(lax.axis_size("a"), 4, lax.axis_size("h"), 2 * rows, width)
    view = scatter_step(view, "a", 0)
    view = scatter_step(view, "h", 1)
    owned = lax.all_to_all(view.reshape(8, rows, width).astype(BF), TEAM, 0, 0, tiled=True)
    return owned.transpose(1, 0, 2).astype(F32)


def rows_scatter(partial, rows):
    view = partial.reshape(lax.axis_size("a"), 2, 2, lax.axis_size("h"), 2, rows, -1)
    view = scatter_step(view, "c", 2)
    view = scatter_step(view, "b", 1)
    view = scatter_step(view, "l", 2)
    view = scatter_step(view, "a", 0)
    return scatter_step(view, "h", 0)


def dot(a, b, over):
    return lax.dot_general(a, b, ((over[0], over[1]), ((), ())), preferred_element_type=F32)


NN = ((1,), (0,))
NT = ((1,), (1,))
TN = ((0,), (0,))


def softmax_parts(late, length, q, keys, early_keys):
    rows = q.shape[0]
    slot = late * rows + lax.broadcasted_iota(jnp.int32, (rows, rows), 0)
    key_slot = late * rows + lax.broadcasted_iota(jnp.int32, (rows, rows), 1)
    allowed = (key_slot <= slot) & (key_slot < length)
    own = jnp.where(allowed, dot(q, keys, NT) * SIZE**-0.5, -1e30)
    early_slot = lax.broadcasted_iota(jnp.int32, (rows, rows), 1)
    early = jnp.where(
        (early_slot < late * rows) & (early_slot < length), dot(q, early_keys, NT) * SIZE**-0.5, -1e30
    )
    peak = jnp.maximum(
        jnp.max(own, axis=-1, keepdims=True), jnp.max(early, axis=-1, keepdims=True)
    )
    own, early = jnp.exp(own - peak), jnp.exp(early - peak)
    total = jnp.sum(own, axis=-1, keepdims=True) + jnp.sum(early, axis=-1, keepdims=True)
    part = 1.0 / total
    return own * part, early * part


def forward_kernel(late_ref, length_ref, q_ref, k_ref, v_ref, ek_ref, ev_ref, o_ref):
    late, length = late_ref[0], length_ref[pl.program_id(0)]
    outs = []
    for head in range(SHARE):
        q = q_ref[0, :, head * SIZE : (head + 1) * SIZE]
        own, early = softmax_parts(late, length, q, k_ref[0], ek_ref[0])
        outs.append(dot(own.astype(BF), v_ref[0], NN) + dot(early.astype(BF), ev_ref[0], NN))
    o_ref[0] = jnp.concatenate(outs, axis=-1).astype(BF)


def backward_kernel(
    late_ref, length_ref, q_ref, k_ref, v_ref, ek_ref, ev_ref, g_ref, dq_ref, dk_ref, dv_ref, edk_ref, edv_ref
):
    late, length = late_ref[0], length_ref[pl.program_id(0)]
    scale = SIZE**-0.5
    dqs = []
    dk = dv = edk = edv = 0.0
    for head in range(SHARE):
        q = q_ref[0, :, head * SIZE : (head + 1) * SIZE]
        g = g_ref[0, :, head * SIZE : (head + 1) * SIZE]
        own, early = softmax_parts(late, length, q, k_ref[0], ek_ref[0])
        dp, edp = dot(g, v_ref[0], NT), dot(g, ev_ref[0], NT)
        inner = jnp.sum(own * dp, axis=-1, keepdims=True) + jnp.sum(
            early * edp, axis=-1, keepdims=True
        )
        ds = (own * (dp - inner)).astype(BF)
        eds = (early * (edp - inner)).astype(BF)
        dqs.append((dot(ds, k_ref[0], NN) + dot(eds, ek_ref[0], NN)) * scale)
        dv = dv + dot(own.astype(BF), g, TN)
        edv = edv + dot(early.astype(BF), g, TN)
        dk = dk + dot(ds, q, TN)
        edk = edk + dot(eds, q, TN)
    dq_ref[0] = jnp.concatenate(dqs, axis=-1)
    dk_ref[0], dv_ref[0] = dk * scale, dv
    edk_ref[0], edv_ref[0] = (edk * scale).astype(BF), edv.astype(BF)


def attention_call(kernel, late, lengths, arrays, outs, flops):
    count, rows, _ = arrays[0].shape

    def spec(width):
        return pl.BlockSpec((1, rows, width), lambda s, *_: (s, 0, 0))

    return pl.pallas_call(
        kernel,
        grid_spec=pltpu.PrefetchScalarGridSpec(
            num_scalar_prefetch=2,
            grid=(count,),
            in_specs=[spec(x.shape[-1]) for x in arrays],
            out_specs=[spec(width) for width, _ in outs],
        ),
        out_shape=[jax.ShapeDtypeStruct((count, rows, width), kind) for width, kind in outs],
        compiler_params=pltpu.CompilerParams(vmem_limit_bytes=48 * 2**20),
        cost_estimate=pl.CostEstimate(flops=flops, bytes_accessed=8 * 2**20, transcendentals=2**23),
    )(late, lengths, *arrays)


def norm_parts(value):
    return lax.rsqrt(jnp.mean(value * value, axis=-1, keepdims=True) + EPS)


def norm_back(value, gain, grad):
    r = norm_parts(value)
    hat = value * r
    scaled = grad * gain
    return r * (scaled - hat * jnp.mean(scaled * hat, axis=-1, keepdims=True)), hat


def local(
    inputs,
    lengths,
    positions,
    attn_gain,
    w_query,
    w_key,
    w_value,
    w_output,
    ffn_gain,
    w_gate,
    w_up,
    w_down,
    out_grad,
):
    _, slots, width = inputs.shape
    rows = w_gate.shape[0]
    h, l = lax.axis_index("h"), lax.axis_index("l")
    half = 2 * slots
    own_slot = (h * 2 + l) * slots + jnp.arange(slots, dtype=jnp.int32)
    valid = (own_slot < lengths[0])[:, None]
    own = inputs[0]
    grad_out = jnp.where(valid, out_grad[0], jnp.zeros((), BF))

    gains = lax.all_gather(jnp.stack([attn_gain, ffn_gain]), EVERY, axis=1, tiled=True).astype(F32)
    attn_gain_full, ffn_gain_full = gains[0], gains[1]
    team_inputs = lax.all_gather(own, TEAM, axis=0, tiled=True)
    team_positions = lax.all_gather(positions[0], TEAM, axis=0, tiled=True)
    team_lengths = lax.all_gather(lengths, ("b", "c"), axis=0, tiled=True)
    w_qkv = gather_slices(
        jnp.concatenate([slices_of(w, rows) for w in (w_query, w_key, w_value)], axis=-1)
    )
    cosine, sine = rope_tables(team_positions)

    team_f = team_inputs.astype(F32)
    normed_attn = (team_f * norm_parts(team_f) * attn_gain_full).astype(BF)
    qkv = dot(normed_attn, w_qkv, NN)
    q_width = SHARE * SIZE
    tokens = qkv.shape[0]
    query = rotate(
        qkv[:, :q_width].reshape(tokens, SHARE, SIZE), cosine[:, None], sine[:, None]
    ).astype(BF)
    query = query.reshape(4, half, q_width)
    keys = rotate(qkv[:, q_width : q_width + SIZE], cosine, sine).astype(BF).reshape(4, half, SIZE)
    values = qkv[:, q_width + SIZE :].astype(BF).reshape(4, half, SIZE)
    early = lax.ppermute(jnp.stack([keys, values]), "h", [(0, 1)])
    attention_in = (query, keys, values, early[0], early[1])
    late = h.astype(jnp.int32).reshape(1)
    attended = attention_call(
        forward_kernel, late, team_lengths, attention_in, [(q_width, BF)], 3 * 10**9
    )[0]
    attended = lax.all_to_all(attended.reshape(8, slots, q_width), TEAM, 0, 0, tiled=True)
    attended = attended.transpose(1, 0, 2).reshape(slots, HEADS * SIZE)

    w_out = lax.all_gather(w_output, EVERY, axis=0, tiled=True)
    hidden = own.astype(F32) + dot(attended, w_out, NN)
    normed_ffn = (hidden * norm_parts(hidden) * ffn_gain_full).astype(BF)

    team_grad = lax.all_gather(grad_out, TEAM, axis=0, tiled=True)
    gate_w = gather_slices(slices_of(w_gate, rows))
    up_w = gather_slices(slices_of(w_up, rows))
    down_w = gather_slices(slices_of(w_down, rows))
    team_ffn = lax.all_gather(normed_ffn, TEAM, axis=0, tiled=True)
    gate = dot(team_ffn, gate_w, NN)
    up = dot(team_ffn, up_w, NN)
    sigmoid = jax.nn.sigmoid(gate)
    silu = gate * sigmoid
    activated = (silu * up).astype(BF)
    grad_act = dot(team_grad, down_w, NN)
    grad_gate = (grad_act * up * sigmoid * (1.0 + gate * (1.0 - sigmoid))).astype(BF)
    grad_up = (grad_act * silu).astype(BF)
    grad_nffn = team_scatter(dot(grad_gate, gate_w, NT) + dot(grad_up, up_w, NT))
    down_out = team_scatter(dot(activated, down_w, NT))
    output = jnp.where(valid, hidden + down_out, 0.0).astype(BF)
    gate_grad = scatter_slices(dot(team_ffn, grad_gate, TN), rows).reshape(rows, -1)
    up_grad = scatter_slices(dot(team_ffn, grad_up, TN), rows).reshape(rows, -1)
    down_grad = scatter_slices(dot(team_grad, activated, TN), rows).reshape(rows, -1)

    grad_hidden, hat = norm_back(hidden, ffn_gain_full, grad_nffn)
    grad_hidden = grad_hidden + grad_out.astype(F32)
    ffn_gain_term = jnp.sum(grad_nffn * hat, axis=0)

    grad_branch = grad_hidden.astype(BF)
    output_grad = rows_scatter(dot(attended, grad_branch, TN), rows)
    grad_attended = dot(grad_branch, w_out, NT).astype(BF)
    grad_heads = lax.all_to_all(
        grad_attended.reshape(slots, 8, q_width).transpose(1, 0, 2), TEAM, 0, 0, tiled=True
    ).reshape(4, half, q_width)
    grad_query, grad_keys, grad_values, grad_ek, grad_ev = attention_call(
        backward_kernel,
        late,
        team_lengths,
        attention_in + (grad_heads,),
        [(q_width, F32), (SIZE, F32), (SIZE, F32), (SIZE, BF), (SIZE, BF)],
        8 * 10**9,
    )
    back = lax.ppermute(jnp.stack([grad_ek, grad_ev]), "h", [(1, 0)]).astype(F32)
    grad_q = rotate_back(
        grad_query.reshape(tokens, SHARE, SIZE), cosine[:, None], sine[:, None]
    ).reshape(tokens, q_width)
    grad_k = rotate_back((grad_keys + back[0]).reshape(tokens, SIZE), cosine, sine)
    grad_v = (grad_values + back[1]).reshape(tokens, SIZE)
    grad_qkv = jnp.concatenate([grad_q, grad_k, grad_v], axis=-1).astype(BF)
    partial = dot(grad_qkv, w_qkv, NT)
    qkv_grad = scatter_slices(dot(normed_attn, grad_qkv, TN), rows)
    grad_nattn = team_scatter(partial)
    grad_input, hat = norm_back(own.astype(F32), attn_gain_full, grad_nattn)
    input_grad = (grad_hidden + grad_input).astype(BF)
    attn_gain_term = jnp.sum(grad_nattn * hat, axis=0)
    gain_grads = lax.psum_scatter(
        jnp.stack([attn_gain_term, ffn_gain_term]), EVERY, scatter_dimension=1, tiled=True
    )
    return (
        output[None],
        input_grad[None],
        gain_grads[0],
        qkv_grad[:, :, :q_width].reshape(rows, -1),
        qkv_grad[:, :, q_width : q_width + SIZE].reshape(rows, -1),
        qkv_grad[:, :, q_width + SIZE :].reshape(rows, -1),
        output_grad,
        gain_grads[1],
        gate_grad,
        up_grad,
        down_grad,
    )


def solution(mesh):
    n_dp, n_seq = mesh.shape["dp"], mesh.shape["seq"]
    fine = Mesh(mesh.devices.reshape(n_dp // 4, 2, 2, n_seq // 2, 2), EVERY)
    tokens = P(("a", "b", "c"), ("h", "l"), None)
    matrix = P(EVERY, None)
    vector = P(EVERY)
    placed = (
        tokens,
        P(("a", "b", "c")),
        P(("a", "b", "c"), ("h", "l")),
        vector,
        matrix,
        matrix,
        matrix,
        matrix,
        vector,
        matrix,
        matrix,
        matrix,
        tokens,
    )
    return jax.shard_map(
        local,
        mesh=fine,
        in_specs=placed,
        out_specs=(
            tokens, tokens, vector, matrix, matrix, matrix, matrix, vector, matrix, matrix, matrix
        ),
        check_vma=False,
    )
```

```python
import functools
import math

import jax
import jax.numpy as jnp
from jax import lax
from jax.experimental import pallas as pl
from jax.experimental.pallas import tpu as pltpu
from jax.sharding import Mesh
from jax.sharding import PartitionSpec as P

HEADS = 32
GROUPS = 8
SIZE = 64
SHARE = HEADS // GROUPS
EPS = 1e-05
TEAM = ("b", "c", "l")
EVERY = ("a", "b", "c", "h", "l")
BF = jnp.bfloat16
F32 = jnp.float32


def rope_tables(positions):
    index = jnp.arange(SIZE // 2, dtype=F32)
    frequency = 1.0 / 500000.0 ** (2.0 * index / SIZE)
    wavelength = 2.0 * math.pi / frequency
    blending = (8192.0 / wavelength - 1.0) / (4.0 - 1.0)
    middle = (1.0 - blending) * frequency / 32.0 + blending * frequency
    scaled = jnp.where(
        wavelength < 8192.0 / 4.0,
        frequency,
        jnp.where(wavelength > 8192.0, frequency / 32.0, middle),
    )
    angles = positions.astype(F32)[..., None] * scaled
    angles = jnp.concatenate([angles, angles], axis=-1)
    return jnp.cos(angles), jnp.sin(angles)


def rotate(v, cosine, sine):
    first, second = jnp.split(v, 2, axis=-1)
    return v * cosine + jnp.concatenate([-second, first], axis=-1) * sine


def rotate_back(v, cosine, sine):
    turned = v * sine
    first, second = jnp.split(turned, 2, axis=-1)
    return v * cosine + jnp.concatenate([second, -first], axis=-1)


def shift(value, axis, step):
    n = lax.axis_size(axis)
    return lax.ppermute(value, axis, [(i, (i + step) % n) for i in range(n)])


def scatter_step(value, axis, dim):
    n = lax.axis_size(axis)
    me = lax.axis_index(axis)
    kept = lax.dynamic_index_in_dim(value, me, dim, keepdims=False).astype(F32)
    for s in range(1, n):
        sent = lax.dynamic_index_in_dim(value, lax.rem(me + s, n), dim, keepdims=False)
        kept = kept + shift(sent.astype(BF), axis, s).astype(F32)
    return kept


def team_scatter(partial):
    width = partial.shape[-1]
    view = partial.reshape(2, 2, 2, -1, width)
    view = scatter_step(view, "c", 1)
    left = scatter_step(view[..., : width // 2], "l", 1)
    left = scatter_step(left, "b", 0)
    right = scatter_step(view[..., width // 2 :], "b", 0)
    right = scatter_step(right, "l", 0)
    return jnp.concatenate([left, right], axis=-1)


def slices_of(weight, rows):
    return weight.reshape(rows, 8, -1)


def gather_slices(local):
    rows, _, width = local.shape
    n_a, n_h = lax.axis_size("a"), lax.axis_size("h")
    a, h = lax.axis_index("a"), lax.axis_index("h")
    piece = lax.all_to_all(local.transpose(1, 0, 2), TEAM, 0, 0, tiled=True)
    whole = jnp.zeros((n_a, 4, n_h, 2 * rows, width), local.dtype)
    for dh in range(n_h):
        from_h = shift(piece, "h", -dh) if dh else piece
        for da in range(n_a):
            block = shift(from_h, "a", -da) if da else from_h
            whole = lax.dynamic_update_slice(
                whole,
                block.reshape(1, 4, 1, 2 * rows, width),
                (lax.rem(a + da, n_a), 0, lax.rem(h + dh, n_h), 0, 0),
            )
    return whole.reshape(-1, width)


def scatter_slices(partial, rows):
    width = partial.shape[-1]
    view = partial.reshape(lax.axis_size("a"), 4, lax.axis_size("h"), 2 * rows, width)
    view = scatter_step(view, "a", 0)
    view = scatter_step(view, "h", 1)
    owned = lax.all_to_all(view.reshape(8, rows, width).astype(BF), TEAM, 0, 0, tiled=True)
    return owned.transpose(1, 0, 2).astype(F32)


def relative_scatter(partial):
    half = partial.shape[-1] // 2

    def fold(value, axis, dim):
        kept = lax.index_in_dim(value, 0, dim, keepdims=False).astype(F32)
        sent = lax.index_in_dim(value, 1, dim, keepdims=False).astype(BF)
        return kept + shift(sent, axis, 1).astype(F32)

    view = fold(partial, "c", 2)
    left = fold(fold(view[..., :half], "l", 0), "b", 0)
    right = fold(fold(view[..., half:], "b", 1), "l", 0)
    return jnp.concatenate([left, right], axis=-1)


def rows_scatter(partial, rows):
    view = partial.reshape(lax.axis_size("a"), 2, 2, lax.axis_size("h"), 2, rows, -1)
    view = scatter_step(view, "c", 2)
    view = scatter_step(view, "b", 1)
    view = scatter_step(view, "l", 2)
    view = scatter_step(view, "a", 0)
    return scatter_step(view, "h", 0)


def dot(a, b, over):
    return lax.dot_general(a, b, ((over[0], over[1]), ((), ())), preferred_element_type=F32)


NN = ((1,), (0,))
NT = ((1,), (1,))
TN = ((0,), (0,))


def softmax_parts(late, length, q, keys, early_keys):
    rows = q.shape[0]
    slot = late * rows + lax.broadcasted_iota(jnp.int32, (rows, rows), 0)
    key_slot = late * rows + lax.broadcasted_iota(jnp.int32, (rows, rows), 1)
    allowed = (key_slot <= slot) & (key_slot < length)
    own = jnp.where(allowed, dot(q, keys, NT) * SIZE**-0.5, -1e30)
    early_slot = lax.broadcasted_iota(jnp.int32, (rows, rows), 1)
    early = jnp.where(
        (early_slot < late * rows) & (early_slot < length), dot(q, early_keys, NT) * SIZE**-0.5, -1e30
    )
    peak = jnp.maximum(
        jnp.max(own, axis=-1, keepdims=True), jnp.max(early, axis=-1, keepdims=True)
    )
    own, early = jnp.exp(own - peak), jnp.exp(early - peak)
    total = jnp.sum(own, axis=-1, keepdims=True) + jnp.sum(early, axis=-1, keepdims=True)
    part = 1.0 / total
    return own * part, early * part


def forward_kernel(late_ref, length_ref, q_ref, k_ref, v_ref, ek_ref, ev_ref, o_ref):
    late, length = late_ref[0], length_ref[pl.program_id(0)]
    outs = []
    for head in range(SHARE):
        q = q_ref[0, :, head * SIZE : (head + 1) * SIZE]
        own, early = softmax_parts(late, length, q, k_ref[0], ek_ref[0])
        outs.append(dot(own.astype(BF), v_ref[0], NN) + dot(early.astype(BF), ev_ref[0], NN))
    o_ref[0] = jnp.concatenate(outs, axis=-1).astype(BF)


def backward_kernel(
    late_ref, length_ref, q_ref, k_ref, v_ref, ek_ref, ev_ref, g_ref, dq_ref, dk_ref, dv_ref, edk_ref, edv_ref
):
    late, length = late_ref[0], length_ref[pl.program_id(0)]
    scale = SIZE**-0.5
    dqs = []
    dk = dv = edk = edv = 0.0
    for head in range(SHARE):
        q = q_ref[0, :, head * SIZE : (head + 1) * SIZE]
        g = g_ref[0, :, head * SIZE : (head + 1) * SIZE]
        own, early = softmax_parts(late, length, q, k_ref[0], ek_ref[0])
        dp, edp = dot(g, v_ref[0], NT), dot(g, ev_ref[0], NT)
        inner = jnp.sum(own * dp, axis=-1, keepdims=True) + jnp.sum(
            early * edp, axis=-1, keepdims=True
        )
        ds = (own * (dp - inner)).astype(BF)
        eds = (early * (edp - inner)).astype(BF)
        dqs.append((dot(ds, k_ref[0], NN) + dot(eds, ek_ref[0], NN)) * scale)
        dv = dv + dot(own.astype(BF), g, TN)
        edv = edv + dot(early.astype(BF), g, TN)
        dk = dk + dot(ds, q, TN)
        edk = edk + dot(eds, q, TN)
    dq_ref[0] = jnp.concatenate(dqs, axis=-1)
    dk_ref[0], dv_ref[0] = dk * scale, dv
    edk_ref[0], edv_ref[0] = (edk * scale).astype(BF), edv.astype(BF)


def attention_call(kernel, late, lengths, arrays, outs, flops):
    count, rows, _ = arrays[0].shape

    def spec(width):
        return pl.BlockSpec((1, rows, width), lambda s, *_: (s, 0, 0))

    return pl.pallas_call(
        kernel,
        grid_spec=pltpu.PrefetchScalarGridSpec(
            num_scalar_prefetch=2,
            grid=(count,),
            in_specs=[spec(x.shape[-1]) for x in arrays],
            out_specs=[spec(width) for width, _ in outs],
        ),
        out_shape=[jax.ShapeDtypeStruct((count, rows, width), kind) for width, kind in outs],
        compiler_params=pltpu.CompilerParams(vmem_limit_bytes=48 * 2**20),
        cost_estimate=pl.CostEstimate(flops=flops, bytes_accessed=8 * 2**20, transcendentals=2**23),
    )(late, lengths, *arrays)


MESH = pl.DeviceIdType.MESH


def ffn_kernel(
    own_ref,
    grad_ref,
    wg_ref,
    wu_ref,
    wd_ref,
    gn_ref,
    dn_ref,
    dwg_ref,
    dwu_ref,
    dwd_ref,
    wg,
    wu,
    wd,
    xs,
    gs,
    act,
    gg,
    gu,
    send_sib,
    recv_sib,
    send_own,
    recv_own,
    stage,
    local_sem,
    grad_sem,
    ag_send,
    ag_recv,
    sib_send,
    sib_recv,
    own_send,
    own_recv,
    stage_sem,
    credit,
):
    b, c, l = lax.axis_index("b"), lax.axis_index("c"), lax.axis_index("l")
    rows, width = own_ref.shape
    tile = wg.shape[1]
    sibling = {"c": 1 - c}

    def chip(k):
        return {"b": lax.rem(b + lax.rem(k, 2), 2), "l": lax.rem(l + k // 2, 2)}

    barrier = pltpu.get_barrier_semaphore()
    for peer in (sibling, chip(1), chip(2), chip(3)):
        pl.semaphore_signal(barrier, inc=1, device_id=peer, device_id_type=MESH)
    pl.semaphore_wait(barrier, 4)

    def part(slot):
        return pl.ds(pl.multiple_of(slot * rows, rows), rows)

    def gather_copy(source, slot, peer):
        return pltpu.make_async_remote_copy(
            src_ref=source,
            dst_ref=xs.at[part(slot)],
            send_sem=ag_send.at[slot],
            recv_sem=ag_recv.at[slot],
            device_id=peer,
            device_id_type=MESH,
        )

    def forward_copy(k):
        return gather_copy(xs.at[part(2 * k)], 2 * k + 1, sibling)

    def sibling_copy(k):
        spot = lax.rem(k, 2)
        return pltpu.make_async_remote_copy(
            src_ref=send_sib.at[spot],
            dst_ref=recv_sib.at[spot],
            send_sem=sib_send.at[spot],
            recv_sem=sib_recv.at[spot],
            device_id=sibling,
            device_id_type=MESH,
        )

    def owner_copy(k):
        return pltpu.make_async_remote_copy(
            src_ref=send_own.at[k - 1],
            dst_ref=recv_own.at[k - 1],
            send_sem=own_send.at[k - 1],
            recv_sem=own_recv.at[k - 1],
            device_id=chip(k),
            device_id_type=MESH,
        )

    def grad_copy(slot):
        k, dc = slot // 2, lax.rem(slot, 2)
        db, dl = lax.rem(k, 2), k // 2
        source = (lax.rem(b + db, 2) * 2 + lax.rem(c + dc, 2)) * 2 + lax.rem(l + dl, 2)
        return pltpu.make_async_copy(grad_ref.at[source], gs.at[part(slot)], grad_sem.at[slot])

    def down_copy(spot, slot):
        cols = pl.ds(spot * tile, tile)
        return pltpu.make_async_copy(stage.at[spot], dn_ref.at[slot, :, cols], stage_sem.at[spot])

    gather_copy(own_ref, 1, sibling).start()
    for k in (1, 2, 3):
        gather_copy(own_ref, 2 * k, chip(k)).start()
    own_copy = pltpu.make_async_copy(own_ref, xs.at[part(0)], local_sem.at[0])
    own_copy.start()
    loads = [
        pltpu.make_async_copy(source, target, local_sem.at[1 + j])
        for j, (source, target) in enumerate(((wg_ref, wg), (wu_ref, wu), (wd_ref, wd)))
    ]
    for load in loads:
        load.start()
    for slot in range(8):
        grad_copy(slot).start()
    for load in loads:
        load.wait()
    own_copy.wait()

    def block(i, carry):
        k, second = i // 2, lax.rem(i, 2)
        slot = 2 * k + 1 - second
        spot = lax.rem(k, 2)
        for at, ready in ((2, 1), (3, 2), (5, 3)):

            @pl.when(i == at)
            def _():
                gather_copy(own_ref, 2 * ready, chip(ready)).wait_recv()
                forward_copy(ready).start()

        @pl.when(second == 0)
        def _():
            gather_copy(own_ref, slot, sibling).wait_recv()

        grad_copy(slot).wait()
        for piece in (slice(0, tile // 2), slice(tile // 2, tile)):
            gate = dot(xs[part(slot), :], wg[:, piece], NN)
            up = dot(xs[part(slot), :], wu[:, piece], NN)
            grad_act = dot(gs[part(slot), :], wd[:, piece], NN)
            sigmoid = jax.nn.sigmoid(gate)
            silu = gate * sigmoid
            act[part(slot), piece] = (silu * up).astype(BF)
            gu[part(slot), piece] = (grad_act * silu).astype(BF)
            slope = sigmoid * (1.0 + gate * (1.0 - sigmoid))
            gg[part(slot), piece] = (grad_act * up * slope).astype(BF)

        @pl.when((second == 0) & (k >= 2))
        def _():
            sibling_copy(k).wait_send()

        @pl.when(second == 1)
        def _():
            sibling_copy(k).wait_recv()

        for start in range(0, width, tile):
            cols = slice(start, start + tile)
            part_gn = dot(gg[part(slot), :], wg[cols, :], NT)
            part_gn += dot(gu[part(slot), :], wu[cols, :], NT)

            @pl.when(second == 0)
            def _():
                send_sib[spot, :, cols] = part_gn.astype(BF)

            @pl.when(i == 1)
            def _():
                gn_ref[:, cols] = part_gn + recv_sib[spot, :, cols].astype(F32)

            @pl.when((second == 1) & (k > 0))
            def _():
                send_own[k - 1, :, cols] = (part_gn + recv_sib[spot, :, cols].astype(F32)).astype(BF)

        @pl.when((second == 0) & (k >= 2))
        def _():
            pl.semaphore_wait(credit, 1)

        @pl.when(second == 0)
        def _():
            sibling_copy(k).start()

        @pl.when((second == 1) & (k < 2))
        def _():
            pl.semaphore_signal(credit, inc=1, device_id=sibling, device_id_type=MESH)

        @pl.when((second == 1) & (k > 0))
        def _():
            owner_copy(k).start()

        for at in range(width // tile):
            part_dn = dot(act[part(slot), :], wd[at * tile : (at + 1) * tile, :], NT)

            @pl.when(i >= 1)
            def _():
                down_copy(at, slot).wait()

            stage[at] = part_dn.astype(BF)
            down_copy(at, slot).start()
        return carry

    lax.fori_loop(0, 8, block, 0)
    for at in range(width // tile):
        down_copy(at, 0).wait()

    step = rows

    def weight_copy(j, which, target):
        return pltpu.make_async_copy(
            stage.at[which],
            target.at[pl.ds(pl.multiple_of(j * step, step), step)],
            stage_sem.at[which],
        )

    def weights(j, carry):
        cols = pl.ds(pl.multiple_of(j * step, step), step)
        for which, (left, right, target) in enumerate(
            ((xs, gg, dwg_ref), (xs, gu, dwu_ref), (gs, act, dwd_ref))
        ):

            @pl.when(j > 0)
            def _():
                weight_copy(j, which, target).wait()

            stage[which] = dot(left[:, cols], right[...], TN).astype(BF)
            weight_copy(j, which, target).start()
        return carry

    lax.fori_loop(0, width // step, weights, 0)

    for k in (1, 2, 3):
        owner_copy(k).wait_recv()
        gn_ref[...] += recv_own[k - 1].astype(F32)
    for which, target in enumerate((dwg_ref, dwu_ref, dwd_ref)):
        weight_copy(0, which, target).wait()
    for k in (0, 1):
        sibling_copy(k).wait_send()
    gather_copy(own_ref, 1, sibling).wait_send()
    for k in (1, 2, 3):
        gather_copy(own_ref, 2 * k, chip(k)).wait_send()
        forward_copy(k).wait_send()
        owner_copy(k).wait_send()


def ffn_call(own, team_grad, gate_w, up_w, down_w):
    rows, width = own.shape
    hidden = gate_w.shape[1]
    team = 8 * rows
    anywhere = pl.BlockSpec(memory_space=pl.ANY)
    stages = max(3, width // hidden)
    return pl.pallas_call(
        ffn_kernel,
        in_specs=[anywhere] * 5,
        out_specs=[pl.BlockSpec(memory_space=pltpu.VMEM)] + [anywhere] * 4,
        out_shape=[
            jax.ShapeDtypeStruct((rows, width), F32),
            jax.ShapeDtypeStruct((8, rows, width), BF),
        ]
        + [jax.ShapeDtypeStruct((width, hidden), BF)] * 3,
        scratch_shapes=[pltpu.VMEM((width, hidden), BF)] * 3
        + [pltpu.VMEM((team, width), BF)] * 2
        + [pltpu.VMEM((team, hidden), BF)] * 3
        + [pltpu.VMEM((2, rows, width), BF)] * 2
        + [pltpu.VMEM((3, rows, width), BF)] * 2
        + [pltpu.VMEM((stages, rows, hidden), BF)]
        + [pltpu.SemaphoreType.DMA((n,)) for n in (4, 8, 8, 8, 2, 2, 3, 3, stages)]
        + [pltpu.SemaphoreType.REGULAR],
        compiler_params=pltpu.CompilerParams(
            collective_id=0, has_side_effects=True, vmem_limit_bytes=60 * 2**20
        ),
        cost_estimate=pl.CostEstimate(
            flops=18 * team * width * hidden, bytes_accessed=60 * 2**20, transcendentals=team * hidden
        ),
    )(own, team_grad, gate_w, up_w, down_w)


def norm_parts(value):
    return lax.rsqrt(jnp.mean(value * value, axis=-1, keepdims=True) + EPS)


def norm_back(value, gain, grad):
    r = norm_parts(value)
    hat = value * r
    scaled = grad * gain
    return r * (scaled - hat * jnp.mean(scaled * hat, axis=-1, keepdims=True)), hat


def local(
    inputs,
    lengths,
    positions,
    attn_gain,
    w_query,
    w_key,
    w_value,
    w_output,
    ffn_gain,
    w_gate,
    w_up,
    w_down,
    out_grad,
):
    _, slots, width = inputs.shape
    rows = w_gate.shape[0]
    h, l = lax.axis_index("h"), lax.axis_index("l")
    half = 2 * slots
    own_slot = (h * 2 + l) * slots + jnp.arange(slots, dtype=jnp.int32)
    valid = (own_slot < lengths[0])[:, None]
    own = inputs[0]
    grad_out = jnp.where(valid, out_grad[0], jnp.zeros((), BF))

    gains = lax.all_gather(jnp.stack([attn_gain, ffn_gain]), EVERY, axis=1, tiled=True).astype(F32)
    attn_gain_full, ffn_gain_full = gains[0], gains[1]
    team_inputs = lax.all_gather(own, TEAM, axis=0, tiled=True)
    team_positions = lax.all_gather(positions[0], TEAM, axis=0, tiled=True)
    team_lengths = lax.all_gather(lengths, ("b", "c"), axis=0, tiled=True)
    w_qkv = gather_slices(
        jnp.concatenate([slices_of(w, rows) for w in (w_query, w_key, w_value)], axis=-1)
    )
    cosine, sine = rope_tables(team_positions)

    team_f = team_inputs.astype(F32)
    normed_attn = (team_f * norm_parts(team_f) * attn_gain_full).astype(BF)
    qkv = dot(normed_attn, w_qkv, NN)
    q_width = SHARE * SIZE
    tokens = qkv.shape[0]
    query = rotate(
        qkv[:, :q_width].reshape(tokens, SHARE, SIZE), cosine[:, None], sine[:, None]
    ).astype(BF)
    query = query.reshape(4, half, q_width)
    keys = rotate(qkv[:, q_width : q_width + SIZE], cosine, sine).astype(BF).reshape(4, half, SIZE)
    values = qkv[:, q_width + SIZE :].astype(BF).reshape(4, half, SIZE)
    early = lax.ppermute(jnp.stack([keys, values]), "h", [(0, 1)])
    attention_in = (query, keys, values, early[0], early[1])
    late = h.astype(jnp.int32).reshape(1)
    attended = attention_call(
        forward_kernel, late, team_lengths, attention_in, [(q_width, BF)], 3 * 10**9
    )[0]
    attended = lax.all_to_all(attended.reshape(8, slots, q_width), TEAM, 0, 0, tiled=True)
    attended = attended.transpose(1, 0, 2).reshape(slots, HEADS * SIZE)

    w_out = lax.all_gather(w_output, EVERY, axis=0, tiled=True)
    hidden = own.astype(F32) + dot(attended, w_out, NN)
    normed_ffn = (hidden * norm_parts(hidden) * ffn_gain_full).astype(BF)

    team_grad = lax.all_gather(grad_out, TEAM, axis=0, tiled=True)
    gate_w = gather_slices(slices_of(w_gate, rows))
    up_w = gather_slices(slices_of(w_up, rows))
    down_w = gather_slices(slices_of(w_down, rows))
    grad_nffn, down_part, gate_dw, up_dw, down_dw = ffn_call(
        normed_ffn, team_grad.reshape(8, slots, width), gate_w, up_w, down_w
    )
    down_out = relative_scatter(down_part.reshape(2, 2, 2, slots, width))
    output = jnp.where(valid, hidden + down_out, 0.0).astype(BF)
    gate_grad = scatter_slices(gate_dw, rows).reshape(rows, -1)
    up_grad = scatter_slices(up_dw, rows).reshape(rows, -1)
    down_grad = scatter_slices(down_dw, rows).reshape(rows, -1)

    grad_hidden, hat = norm_back(hidden, ffn_gain_full, grad_nffn)
    grad_hidden = grad_hidden + grad_out.astype(F32)
    ffn_gain_term = jnp.sum(grad_nffn * hat, axis=0)

    grad_branch = grad_hidden.astype(BF)
    output_grad = rows_scatter(dot(attended, grad_branch, TN), rows)
    grad_attended = dot(grad_branch, w_out, NT).astype(BF)
    grad_heads = lax.all_to_all(
        grad_attended.reshape(slots, 8, q_width).transpose(1, 0, 2), TEAM, 0, 0, tiled=True
    ).reshape(4, half, q_width)
    grad_query, grad_keys, grad_values, grad_ek, grad_ev = attention_call(
        backward_kernel,
        late,
        team_lengths,
        attention_in + (grad_heads,),
        [(q_width, F32), (SIZE, F32), (SIZE, F32), (SIZE, BF), (SIZE, BF)],
        8 * 10**9,
    )
    back = lax.ppermute(jnp.stack([grad_ek, grad_ev]), "h", [(1, 0)]).astype(F32)
    grad_q = rotate_back(
        grad_query.reshape(tokens, SHARE, SIZE), cosine[:, None], sine[:, None]
    ).reshape(tokens, q_width)
    grad_k = rotate_back((grad_keys + back[0]).reshape(tokens, SIZE), cosine, sine)
    grad_v = (grad_values + back[1]).reshape(tokens, SIZE)
    grad_qkv = jnp.concatenate([grad_q, grad_k, grad_v], axis=-1).astype(BF)
    partial = dot(grad_qkv, w_qkv, NT)
    attn_gain_term = jnp.sum(partial * (team_f * norm_parts(team_f)), axis=0)
    extra = jnp.stack([attn_gain_term, ffn_gain_term], axis=-1)
    extra = jnp.pad(extra, ((0, 0), (0, 126)))
    slab = jnp.concatenate([dot(normed_attn, grad_qkv, TN), extra], axis=-1)
    qkv_grad = scatter_slices(slab, rows)
    grad_nattn = team_scatter(partial)
    grad_input, _ = norm_back(own.astype(F32), attn_gain_full, grad_nattn)
    input_grad = (grad_hidden + grad_input).astype(BF)
    q_end, k_end, v_end = q_width, q_width + SIZE, q_width + 2 * SIZE
    gain_grads = jnp.sum(qkv_grad[:, :, v_end : v_end + 2], axis=1)
    return (
        output[None],
        input_grad[None],
        gain_grads[:, 0],
        qkv_grad[:, :, :q_end].reshape(rows, -1),
        qkv_grad[:, :, q_end:k_end].reshape(rows, -1),
        qkv_grad[:, :, k_end:v_end].reshape(rows, -1),
        output_grad,
        gain_grads[:, 1],
        gate_grad,
        up_grad,
        down_grad,
    )


def solution(mesh):
    n_dp, n_seq = mesh.shape["dp"], mesh.shape["seq"]
    fine = Mesh(mesh.devices.reshape(n_dp // 4, 2, 2, n_seq // 2, 2), EVERY)
    tokens = P(("a", "b", "c"), ("h", "l"), None)
    matrix = P(EVERY, None)
    vector = P(EVERY)
    placed = (
        tokens,
        P(("a", "b", "c")),
        P(("a", "b", "c"), ("h", "l")),
        vector,
        matrix,
        matrix,
        matrix,
        matrix,
        vector,
        matrix,
        matrix,
        matrix,
        tokens,
    )
    return jax.shard_map(
        local,
        mesh=fine,
        in_specs=placed,
        out_specs=(
            tokens, tokens, vector, matrix, matrix, matrix, matrix, vector, matrix, matrix, matrix
        ),
        check_vma=False,
    )
```

```python
import functools
import math

import jax
import jax.numpy as jnp
from jax import lax
from jax.experimental import pallas as pl
from jax.experimental.pallas import tpu as pltpu
from jax.sharding import Mesh
from jax.sharding import PartitionSpec as P

HEADS = 32
GROUPS = 8
SIZE = 64
SHARE = HEADS // GROUPS
EPS = 1e-05
TEAM = ("b", "c", "l")
EVERY = ("a", "b", "c", "h", "l")
BF = jnp.bfloat16
F32 = jnp.float32


def rope_tables(positions):
    index = jnp.arange(SIZE // 2, dtype=F32)
    frequency = 1.0 / 500000.0 ** (2.0 * index / SIZE)
    wavelength = 2.0 * math.pi / frequency
    blending = (8192.0 / wavelength - 1.0) / (4.0 - 1.0)
    middle = (1.0 - blending) * frequency / 32.0 + blending * frequency
    scaled = jnp.where(
        wavelength < 8192.0 / 4.0,
        frequency,
        jnp.where(wavelength > 8192.0, frequency / 32.0, middle),
    )
    angles = positions.astype(F32)[..., None] * scaled
    angles = jnp.concatenate([angles, angles], axis=-1)
    return jnp.cos(angles), jnp.sin(angles)


def rope_lanes(cosine, sine):
    signed = jnp.where(jnp.arange(SIZE) < SIZE // 2, -sine, sine)
    ones, zeros = jnp.ones_like(cosine), jnp.zeros_like(sine)
    return (
        jnp.concatenate([cosine, cosine, cosine, ones], axis=-1),
        jnp.concatenate([signed, signed, signed, zeros], axis=-1),
    )


def swap_halves(v):
    lane = lax.broadcasted_iota(jnp.int32, v.shape, 1)
    low = lax.rem(lane, SIZE) < SIZE // 2
    return jnp.where(low, pltpu.roll(v, 128 - SIZE // 2, 1), pltpu.roll(v, SIZE // 2, 1))


def rope_blocks(v, cosine, sine, sign):
    outs = []
    for n in range(3):
        block = v[:, n * 128 : (n + 1) * 128]
        cols = slice(128, 256) if n == 2 else slice(0, 128)
        outs.append(block * cosine[:, cols] + sign * swap_halves(block) * sine[:, cols])
    return jnp.concatenate(outs, axis=-1)


def shift(value, axis, step):
    n = lax.axis_size(axis)
    return lax.ppermute(value, axis, [(i, (i + step) % n) for i in range(n)])


def scatter_step(value, axis, dim):
    n = lax.axis_size(axis)
    me = lax.axis_index(axis)
    kept = lax.dynamic_index_in_dim(value, me, dim, keepdims=False).astype(F32)
    for s in range(1, n):
        sent = lax.dynamic_index_in_dim(value, lax.rem(me + s, n), dim, keepdims=False)
        kept = kept + shift(sent.astype(BF), axis, s).astype(F32)
    return kept


def team_scatter(partial):
    width = partial.shape[-1]
    view = partial.reshape(2, 2, 2, -1, width)
    view = scatter_step(view, "c", 1)
    left = scatter_step(view[..., : width // 2], "l", 1)
    left = scatter_step(left, "b", 0)
    right = scatter_step(view[..., width // 2 :], "b", 0)
    right = scatter_step(right, "l", 0)
    return jnp.concatenate([left, right], axis=-1)


def together(*values):
    return lax.optimization_barrier(values)


def fold_a(partial, rows):
    view = partial.reshape(lax.axis_size("a"), 4, lax.axis_size("h"), 2 * rows, partial.shape[-1])
    return scatter_step(view, "a", 0)


def fold_team(view, rows):
    owned = lax.all_to_all(
        view.reshape(8, rows, view.shape[-1]).astype(BF), TEAM, 0, 0, tiled=True
    )
    return owned.transpose(1, 0, 2).astype(F32)


def relative_scatter(partial):
    half = partial.shape[-1] // 2

    def fold(value, axis, dim):
        kept = lax.index_in_dim(value, 0, dim, keepdims=False).astype(F32)
        sent = lax.index_in_dim(value, 1, dim, keepdims=False).astype(BF)
        return kept + shift(sent, axis, 1).astype(F32)

    view = fold(partial, "c", 2)
    left = fold(fold(view[..., :half], "l", 0), "b", 0)
    right = fold(fold(view[..., half:], "b", 1), "l", 0)
    return jnp.concatenate([left, right], axis=-1)


def rows_scatter(partial, rows):
    view = partial.reshape(lax.axis_size("a"), 2, 2, lax.axis_size("h"), 2, rows, -1)
    view = scatter_step(view, "c", 2)
    view = scatter_step(view, "b", 1)
    view = scatter_step(view, "l", 2)
    view = scatter_step(view, "a", 0)
    return scatter_step(view, "h", 0)


def dot(a, b, over):
    return lax.dot_general(a, b, ((over[0], over[1]), ((), ())), preferred_element_type=F32)


NN = ((1,), (0,))
NT = ((1,), (1,))
TN = ((0,), (0,))


def softmax_parts(late, length, q, keys, early_keys):
    rows = q.shape[0]
    slot = late * rows + lax.broadcasted_iota(jnp.int32, (rows, rows), 0)
    key_slot = late * rows + lax.broadcasted_iota(jnp.int32, (rows, rows), 1)
    allowed = (key_slot <= slot) & (key_slot < length)
    own = jnp.where(allowed, dot(q, keys, NT) * SIZE**-0.5, -1e30)
    early_slot = lax.broadcasted_iota(jnp.int32, (rows, rows), 1)
    early = jnp.where(
        (early_slot < late * rows) & (early_slot < length), dot(q, early_keys, NT) * SIZE**-0.5, -1e30
    )
    peak = jnp.maximum(
        jnp.max(own, axis=-1, keepdims=True), jnp.max(early, axis=-1, keepdims=True)
    )
    own, early = jnp.exp(own - peak), jnp.exp(early - peak)
    total = jnp.sum(own, axis=-1, keepdims=True) + jnp.sum(early, axis=-1, keepdims=True)
    part = 1.0 / total
    return own * part, early * part


Q_END, K_END, V_END = SHARE * SIZE, SHARE * SIZE + SIZE, SHARE * SIZE + 2 * SIZE


def project_kernel(x_ref, gain_ref, w_ref, cos_ref, sin_ref, normed_ref, out_ref):
    x = x_ref[0].astype(F32)
    normed = (x * norm_parts(x) * gain_ref[...]).astype(BF)
    normed_ref[...] = normed
    qkv = dot(normed, w_ref[...], NN)
    out_ref[...] = rope_blocks(qkv, cos_ref[...], sin_ref[...], 1.0).astype(BF)


def project_call(team_packed, gain, w_qkv, cosine, sine):
    _, rows, _ = team_packed.shape
    width = gain.shape[-1]
    return pl.pallas_call(
        project_kernel,
        grid=(8,),
        in_specs=[
            pl.BlockSpec((1, rows, width), lambda i: (i, 0, 0)),
            pl.BlockSpec((1, width), lambda i: (0, 0)),
            pl.BlockSpec((width, V_END), lambda i: (0, 0)),
            pl.BlockSpec((rows, 256), lambda i: (i, 0)),
            pl.BlockSpec((rows, 256), lambda i: (i, 0)),
        ],
        out_specs=[
            pl.BlockSpec((rows, width), lambda i: (i, 0)),
            pl.BlockSpec((rows, V_END), lambda i: (i, 0)),
        ],
        out_shape=[
            jax.ShapeDtypeStruct((8 * rows, width), BF),
            jax.ShapeDtypeStruct((8 * rows, V_END), BF),
        ],
        compiler_params=pltpu.CompilerParams(vmem_limit_bytes=40 * 2**20),
        cost_estimate=pl.CostEstimate(
            flops=16 * rows * width * V_END, bytes_accessed=24 * 2**20, transcendentals=0
        ),
    )(team_packed, gain, w_qkv, cosine, sine)


def unrotate_kernel(own_ref, back_ref, cos_ref, sin_ref, out_ref):
    own = own_ref[...]
    tail = own[:, Q_END:] + back_ref[...].astype(F32)
    total = jnp.concatenate([own[:, :Q_END], tail], axis=-1)
    out_ref[...] = rope_blocks(total, cos_ref[...], sin_ref[...], -1.0).astype(BF)


def unrotate_call(own, back, cosine, sine):
    tokens = own.shape[0]
    rows = tokens // 4

    def spec(x):
        return pl.BlockSpec((rows, x.shape[1]), lambda i: (i, 0))

    return pl.pallas_call(
        unrotate_kernel,
        grid=(4,),
        in_specs=[spec(x) for x in (own, back, cosine, sine)],
        out_specs=spec(own),
        out_shape=jax.ShapeDtypeStruct(own.shape, BF),
        cost_estimate=pl.CostEstimate(flops=10**7, bytes_accessed=9 * 2**20, transcendentals=0),
    )(own, back, cosine, sine)


def forward_kernel(late_ref, length_ref, qkv_ref, early_ref, o_ref):
    late, length = late_ref[0], length_ref[pl.program_id(0)]
    keys, values = qkv_ref[0, :, Q_END:K_END], qkv_ref[0, :, K_END:V_END]
    early_keys, early_values = early_ref[0, :, :SIZE], early_ref[0, :, SIZE:]
    outs = []
    for head in range(SHARE):
        q = qkv_ref[0, :, head * SIZE : (head + 1) * SIZE]
        own, early = softmax_parts(late, length, q, keys, early_keys)
        outs.append(dot(own.astype(BF), values, NN) + dot(early.astype(BF), early_values, NN))
    o_ref[0] = jnp.concatenate(outs, axis=-1).astype(BF)


def backward_kernel(late_ref, length_ref, qkv_ref, early_ref, g_ref, d_ref, ed_ref):
    late, length = late_ref[0], length_ref[pl.program_id(0)]
    keys, values = qkv_ref[0, :, Q_END:K_END], qkv_ref[0, :, K_END:V_END]
    early_keys, early_values = early_ref[0, :, :SIZE], early_ref[0, :, SIZE:]
    scale = SIZE**-0.5
    dqs = []
    dk = dv = edk = edv = 0.0
    for head in range(SHARE):
        q = qkv_ref[0, :, head * SIZE : (head + 1) * SIZE]
        g = g_ref[0, :, head * SIZE : (head + 1) * SIZE]
        own, early = softmax_parts(late, length, q, keys, early_keys)
        dp, edp = dot(g, values, NT), dot(g, early_values, NT)
        inner = jnp.sum(own * dp, axis=-1, keepdims=True) + jnp.sum(
            early * edp, axis=-1, keepdims=True
        )
        ds = (own * (dp - inner)).astype(BF)
        eds = (early * (edp - inner)).astype(BF)
        dqs.append((dot(ds, keys, NN) + dot(eds, early_keys, NN)) * scale)
        dv = dv + dot(own.astype(BF), g, TN)
        edv = edv + dot(early.astype(BF), g, TN)
        dk = dk + dot(ds, q, TN)
        edk = edk + dot(eds, q, TN)
    d_ref[0] = jnp.concatenate(dqs + [dk * scale, dv], axis=-1)
    ed_ref[0] = jnp.concatenate([edk * scale, edv], axis=-1).astype(BF)


def attention_call(kernel, late, lengths, arrays, outs, flops):
    count, rows, _ = arrays[0].shape

    def spec(width):
        return pl.BlockSpec((1, rows, width), lambda s, *_: (s, 0, 0))

    return pl.pallas_call(
        kernel,
        grid_spec=pltpu.PrefetchScalarGridSpec(
            num_scalar_prefetch=2,
            grid=(count,),
            in_specs=[spec(x.shape[-1]) for x in arrays],
            out_specs=[spec(width) for width, _ in outs],
        ),
        out_shape=[jax.ShapeDtypeStruct((count, rows, width), kind) for width, kind in outs],
        compiler_params=pltpu.CompilerParams(vmem_limit_bytes=48 * 2**20),
        cost_estimate=pl.CostEstimate(flops=flops, bytes_accessed=8 * 2**20, transcendentals=2**23),
    )(late, lengths, *arrays)


MESH = pl.DeviceIdType.MESH


def ffn_kernel(
    own_ref,
    grad_ref,
    *refs,
):
    n_pieces = len(refs) - 28
    ffn_body(own_ref, grad_ref, refs[:n_pieces], *refs[n_pieces:])


def ffn_body(
    own_ref,
    grad_ref,
    piece_refs,
    gn_ref,
    dn_ref,
    dwg_ref,
    dwu_ref,
    dwd_ref,
    wg,
    wu,
    wd,
    xs,
    gs,
    act,
    gg,
    gu,
    send_sib,
    recv_sib,
    send_own,
    recv_own,
    stage,
    local_sem,
    grad_sem,
    ag_send,
    ag_recv,
    sib_send,
    sib_recv,
    own_send,
    own_recv,
    stage_sem,
    credit,
):
    b, c, l = lax.axis_index("b"), lax.axis_index("c"), lax.axis_index("l")
    rows, width = own_ref.shape
    tile = wg.shape[1]
    sibling = {"c": 1 - c}

    def chip(k):
        return {"b": lax.rem(b + lax.rem(k, 2), 2), "l": lax.rem(l + k // 2, 2)}

    barrier = pltpu.get_barrier_semaphore()
    for peer in (sibling, chip(1), chip(2), chip(3)):
        pl.semaphore_signal(barrier, inc=1, device_id=peer, device_id_type=MESH)
    pl.semaphore_wait(barrier, 4)

    def part(slot):
        return pl.ds(pl.multiple_of(slot * rows, rows), rows)

    def gather_copy(source, slot, peer):
        return pltpu.make_async_remote_copy(
            src_ref=source,
            dst_ref=xs.at[part(slot)],
            send_sem=ag_send.at[slot],
            recv_sem=ag_recv.at[slot],
            device_id=peer,
            device_id_type=MESH,
        )

    def forward_copy(k):
        return gather_copy(xs.at[part(2 * k)], 2 * k + 1, sibling)

    def sibling_copy(k):
        spot = lax.rem(k, 2)
        return pltpu.make_async_remote_copy(
            src_ref=send_sib.at[spot],
            dst_ref=recv_sib.at[spot],
            send_sem=sib_send.at[spot],
            recv_sem=sib_recv.at[spot],
            device_id=sibling,
            device_id_type=MESH,
        )

    def owner_copy(k):
        return pltpu.make_async_remote_copy(
            src_ref=send_own.at[k - 1],
            dst_ref=recv_own.at[k - 1],
            send_sem=own_send.at[k - 1],
            recv_sem=own_recv.at[k - 1],
            device_id=chip(k),
            device_id_type=MESH,
        )

    def grad_copy(slot):
        k, dc = slot // 2, lax.rem(slot, 2)
        db, dl = lax.rem(k, 2), k // 2
        source = (lax.rem(b + db, 2) * 2 + lax.rem(c + dc, 2)) * 2 + lax.rem(l + dl, 2)
        return pltpu.make_async_copy(grad_ref.at[source], gs.at[part(slot)], grad_sem.at[slot])

    def down_copy(spot, slot):
        cols = pl.ds(spot * tile, tile)
        return pltpu.make_async_copy(stage.at[spot], dn_ref.at[slot, :, cols], stage_sem.at[spot])

    gather_copy(own_ref, 1, sibling).start()
    for k in (1, 2, 3):
        gather_copy(own_ref, 2 * k, chip(k)).start()
    own_copy = pltpu.make_async_copy(own_ref, xs.at[part(0)], local_sem.at[0])
    own_copy.start()
    a, h = lax.axis_index("a"), lax.axis_index("h")
    n_a, n_h = lax.axis_size("a"), lax.axis_size("h")
    chunk = piece_refs[0].shape[1]
    for j, target in enumerate((wg, wu, wd)):
        near, near_a, far, far_a = piece_refs[4 * j : 4 * j + 4]
        for dh, first, rest in ((0, near, near_a), (1, far, far_a)):
            for da in range(n_a):
                source = rest.at[da - 1] if da else first
                ra, rh = lax.rem(a + n_a - da, n_a), lax.rem(h + dh, n_h)
                for pair in range(4):
                    start = pl.multiple_of(((ra * 4 + pair) * n_h + rh) * chunk, chunk)
                    pltpu.make_async_copy(
                        source.at[pair], target.at[pl.ds(start, chunk)], local_sem.at[1 + j]
                    ).start()
    for slot in range(8):
        grad_copy(slot).start()
    for j, target in enumerate((wg, wu, wd)):
        pltpu.make_async_copy(target, target, local_sem.at[1 + j]).wait()
    own_copy.wait()

    def block(i, carry):
        k, second = i // 2, lax.rem(i, 2)
        slot = 2 * k + 1 - second
        spot = lax.rem(k, 2)
        for at, ready in ((2, 1), (3, 2), (5, 3)):

            @pl.when(i == at)
            def _():
                gather_copy(own_ref, 2 * ready, chip(ready)).wait_recv()
                forward_copy(ready).start()

        @pl.when(second == 0)
        def _():
            gather_copy(own_ref, slot, sibling).wait_recv()

        grad_copy(slot).wait()
        for piece in (slice(0, tile // 2), slice(tile // 2, tile)):
            gate = dot(xs[part(slot), :], wg[:, piece], NN)
            up = dot(xs[part(slot), :], wu[:, piece], NN)
            grad_act = dot(gs[part(slot), :], wd[:, piece], NN)
            sigmoid = jax.nn.sigmoid(gate)
            silu = gate * sigmoid
            act[part(slot), piece] = (silu * up).astype(BF)
            gu[part(slot), piece] = (grad_act * silu).astype(BF)
            slope = sigmoid * (1.0 + gate * (1.0 - sigmoid))
            gg[part(slot), piece] = (grad_act * up * slope).astype(BF)

        @pl.when((second == 0) & (k >= 2))
        def _():
            sibling_copy(k).wait_send()

        @pl.when(second == 1)
        def _():
            sibling_copy(k).wait_recv()

        for start in range(0, width, tile):
            cols = slice(start, start + tile)
            part_gn = dot(gg[part(slot), :], wg[cols, :], NT)
            part_gn += dot(gu[part(slot), :], wu[cols, :], NT)

            @pl.when(second == 0)
            def _():
                send_sib[spot, :, cols] = part_gn.astype(BF)

            @pl.when(i == 1)
            def _():
                gn_ref[:, cols] = part_gn + recv_sib[spot, :, cols].astype(F32)

            @pl.when((second == 1) & (k > 0))
            def _():
                send_own[k - 1, :, cols] = (part_gn + recv_sib[spot, :, cols].astype(F32)).astype(BF)

        @pl.when((second == 0) & (k >= 2))
        def _():
            pl.semaphore_wait(credit, 1)

        @pl.when(second == 0)
        def _():
            sibling_copy(k).start()

        @pl.when((second == 1) & (k < 2))
        def _():
            pl.semaphore_signal(credit, inc=1, device_id=sibling, device_id_type=MESH)

        @pl.when((second == 1) & (k > 0))
        def _():
            owner_copy(k).start()

        for at in range(width // tile):
            part_dn = dot(act[part(slot), :], wd[at * tile : (at + 1) * tile, :], NT)

            @pl.when(i >= 1)
            def _():
                down_copy(at, slot).wait()

            stage[at] = part_dn.astype(BF)
            down_copy(at, slot).start()
        return carry

    lax.fori_loop(0, 8, block, 0)
    for at in range(width // tile):
        down_copy(at, 0).wait()

    step = rows

    def weight_copy(j, which, target):
        return pltpu.make_async_copy(
            stage.at[which],
            target.at[pl.ds(pl.multiple_of(j * step, step), step)],
            stage_sem.at[which],
        )

    def weights(j, carry):
        cols = pl.ds(pl.multiple_of(j * step, step), step)
        for which, (left, right, target) in enumerate(
            ((xs, gg, dwg_ref), (xs, gu, dwu_ref), (gs, act, dwd_ref))
        ):

            @pl.when(j > 0)
            def _():
                weight_copy(j, which, target).wait()

            stage[which] = dot(left[:, cols], right[...], TN).astype(BF)
            weight_copy(j, which, target).start()
        return carry

    lax.fori_loop(0, width // step, weights, 0)

    for k in (1, 2, 3):
        owner_copy(k).wait_recv()
        gn_ref[...] += recv_own[k - 1].astype(F32)
    for which, target in enumerate((dwg_ref, dwu_ref, dwd_ref)):
        weight_copy(0, which, target).wait()
    for k in (0, 1):
        sibling_copy(k).wait_send()
    gather_copy(own_ref, 1, sibling).wait_send()
    for k in (1, 2, 3):
        gather_copy(own_ref, 2 * k, chip(k)).wait_send()
        forward_copy(k).wait_send()
        owner_copy(k).wait_send()


def ffn_call(own, team_grad, pieces):
    rows, width = own.shape
    hidden = pieces[0].shape[-1]
    team = 8 * rows
    anywhere = pl.BlockSpec(memory_space=pl.ANY)
    stages = max(3, width // hidden)
    return pl.pallas_call(
        ffn_kernel,
        in_specs=[anywhere] * (2 + len(pieces)),
        out_specs=[pl.BlockSpec(memory_space=pltpu.VMEM)] + [anywhere] * 4,
        out_shape=[
            jax.ShapeDtypeStruct((rows, width), F32),
            jax.ShapeDtypeStruct((8, rows, width), BF),
        ]
        + [jax.ShapeDtypeStruct((width, hidden), BF)] * 3,
        scratch_shapes=[pltpu.VMEM((width, hidden), BF)] * 3
        + [pltpu.VMEM((team, width), BF)] * 2
        + [pltpu.VMEM((team, hidden), BF)] * 3
        + [pltpu.VMEM((2, rows, width), BF)] * 2
        + [pltpu.VMEM((3, rows, width), BF)] * 2
        + [pltpu.VMEM((stages, rows, hidden), BF)]
        + [pltpu.SemaphoreType.DMA((n,)) for n in (4, 8, 8, 8, 2, 2, 3, 3, stages)]
        + [pltpu.SemaphoreType.REGULAR],
        compiler_params=pltpu.CompilerParams(
            collective_id=0, has_side_effects=True, vmem_limit_bytes=60 * 2**20
        ),
        cost_estimate=pl.CostEstimate(
            flops=18 * team * width * hidden, bytes_accessed=60 * 2**20, transcendentals=team * hidden
        ),
    )(own, team_grad, *pieces)


def opening_kernel(
    tok_ref,
    grad_ref,
    qkv_ref,
    gain_ref,
    gate_ref,
    up_ref,
    down_ref,
    toks,
    grads,
    slab,
    gains,
    gate0,
    gate_h,
    gate_a,
    gate_far,
    up0,
    up_h,
    up_a,
    down0,
    down_a,
    team_send,
    team_recv,
    tok_send,
    tok_recv,
    local_sem,
    h_send,
    h_recv,
    a_send,
    a_recv,
):
    a, b, c, h, l = (lax.axis_index(axis) for axis in EVERY)
    n_a = lax.axis_size("a")
    n_rows = qkv_ref.shape[0]
    q_wide, f_wide, g_rows = slab.shape[-1], gate0.shape[-1], gain_ref.shape[0]

    def flip(off):
        return lax.rem(b + off // 4, 2), lax.rem(c + off // 2 % 2, 2), lax.rem(l + off % 2, 2)

    def peer(off):
        pb, pc, p_l = flip(off)
        return {"b": pb, "c": pc, "l": p_l}

    def number(off):
        pb, pc, p_l = flip(off)
        return (pb * 2 + pc) * 2 + p_l

    def a_peer(step):
        return {"a": lax.rem(a + step, n_a)}

    h_peer = {"h": 1 - h}
    barrier = pltpu.get_barrier_semaphore()
    others = [peer(off) for off in range(1, 8)] + [h_peer] + [a_peer(s) for s in range(1, n_a)]
    for other in others:
        pl.semaphore_signal(barrier, inc=1, device_id=other, device_id_type=MESH)
    pl.semaphore_wait(barrier, len(others))

    def source(which, off):
        t = number(off)
        if which == 0:
            return qkv_ref.at[:, pl.ds(pl.multiple_of(t * q_wide, 128), q_wide)]
        if which == 1:
            return gain_ref
        ref = (gate_ref, up_ref, down_ref)[which - 2]
        return ref.at[:, pl.ds(pl.multiple_of(t * f_wide, 128), f_wide)]

    def place(which, off):
        pb, pc, p_l = flip(off)
        pair = pb * 2 + pc
        rows = pl.ds(pl.multiple_of(p_l * n_rows, n_rows), n_rows)
        if which == 0:
            return slab.at[a, pair, h, rows]
        if which == 1:
            return gains.at[a, pair, h, pl.ds(pl.multiple_of(p_l * g_rows, g_rows), g_rows)]
        return (gate0, up0, down0)[which - 2].at[pair, rows]

    def team_copy(which, off, arriving=False):
        return pltpu.make_async_remote_copy(
            src_ref=source(which, off),
            dst_ref=place(which, off if arriving else 0),
            send_sem=team_send.at[which, off],
            recv_sem=team_recv.at[which, off],
            device_id=peer(off),
            device_id_type=MESH,
        )

    def own_copy(which):
        return pltpu.make_async_copy(source(which, 0), place(which, 0), local_sem.at[which])

    def tok_copy(which, from_off, to_off, sem):
        whole = (toks, grads)[which]
        held = (tok_ref, grad_ref)[which] if sem < 6 and sem != 3 else whole.at[number(from_off)]
        return pltpu.make_async_remote_copy(
            src_ref=held,
            dst_ref=whole.at[number(from_off)],
            send_sem=tok_send.at[which, sem],
            recv_sem=tok_recv.at[which, sem],
            device_id=peer(to_off),
            device_id_type=MESH,
        )

    def forward(which, off):
        return tok_copy(which, off, 2, off + 2)

    def region(which, ra, rh):
        if which == 0:
            return slab.at[ra, :, rh]
        return gains.at[ra, :, rh]

    def h_copy(which, arriving=False):
        if which >= 2:
            src, dst = ((gate0, gate_h), (up0, up_h))[which - 2]
        else:
            src = region(which, a, h)
            dst = region(which, a, 1 - h if arriving else h)
        return pltpu.make_async_remote_copy(
            src_ref=src,
            dst_ref=dst,
            send_sem=h_send.at[which],
            recv_sem=h_recv.at[which],
            device_id=h_peer,
            device_id_type=MESH,
        )

    def a_copy(which, step, arriving=False):
        if which >= 4:
            src = (gate0, up0, down0, gate_h)[which - 4]
            dst = (gate_a, up_a, down_a, gate_far)[which - 4].at[step - 1]
        else:
            rh = h if which < 2 else 1 - h
            src = region(which % 2, a, rh)
            dst = region(which % 2, lax.rem(a + n_a - step, n_a) if arriving else a, rh)
        return pltpu.make_async_remote_copy(
            src_ref=src,
            dst_ref=dst,
            send_sem=a_send.at[which, step - 1],
            recv_sem=a_recv.at[which, step - 1],
            device_id=a_peer(step),
            device_id_type=MESH,
        )

    def team_arrived(which):
        own_copy(which).wait()
        for off in range(1, 8):
            team_copy(which, off, arriving=True).wait_recv()

    away = (4, 1, 5)
    steps = range(1, n_a)

    def team_start(*which):
        for w in which:
            for off in range(1, 8):
                team_copy(w, off).start()
            own_copy(w).start()

    def a_start(*which):
        for w in which:
            for step in steps:
                a_copy(w, step).start()

    team_start(0, 1)
    own_toks = [
        pltpu.make_async_copy(src, dst.at[number(0)], local_sem.at[5 + n])
        for n, (src, dst) in enumerate(((tok_ref, toks), (grad_ref, grads)))
    ]
    for which in (0, 1):
        own_toks[which].start()
        tok_copy(which, 0, 2, 2).start()
    team_arrived(0)
    team_arrived(1)
    h_copy(0).start()
    h_copy(1).start()
    a_start(0, 1)
    team_start(2, 3)
    team_arrived(2)
    a_start(4)
    for off in away:
        tok_copy(0, 0, off, off).start()
    team_arrived(3)
    a_start(5)
    team_start(4)
    for which in (0, 1):
        h_copy(which, arriving=True).wait_recv()
    h_copy(2).start()
    a_start(2, 3)
    for off in away:
        tok_copy(0, off, off, off).wait_recv()
        forward(0, off).start()
    for off in away:
        tok_copy(1, 0, off, off).start()
    team_arrived(4)
    a_start(6)
    h_copy(2).wait_recv()
    h_copy(3).start()
    a_start(7)
    for off in away:
        tok_copy(1, off, off, off).wait_recv()
        forward(1, off).start()
    for which in (0, 1):
        own_toks[which].wait()
        tok_copy(which, 2, 2, 2).wait_recv()
        for off in away:
            tok_copy(which, off + 2, 2, off + 2).wait_recv()
    for which in range(8):
        for step in steps:
            a_copy(which, step, arriving=True).wait_recv()
            a_copy(which, step).wait_send()
    h_copy(3).wait_recv()
    for which in range(4):
        h_copy(which).wait_send()
    for which in range(5):
        for off in range(1, 8):
            team_copy(which, off).wait_send()
    for which in (0, 1):
        for off in (2,) + away:
            tok_copy(which, 0, off, off).wait_send()
        for off in away:
            forward(which, off).wait_send()


def opening_call(packed, grad_out, qkv_local, gain_tile, gate, up, down):
    n_a, n_h = lax.axis_size("a"), lax.axis_size("h")
    rows = gate.shape[0]
    q_wide, f_wide = qkv_local.shape[1] // 8, gate.shape[1] // 8
    anywhere = pl.BlockSpec(memory_space=pl.ANY)
    piece = (4, 2 * rows, f_wide)
    shapes = [
        (8,) + packed.shape,
        (8,) + grad_out.shape,
        (n_a, 4, n_h, 2 * rows, q_wide),
        (n_a, 4, n_h, 2 * gain_tile.shape[0], 128),
        piece,
        piece,
        (n_a - 1,) + piece,
        (n_a - 1,) + piece,
        piece,
        piece,
        (n_a - 1,) + piece,
        piece,
        (n_a - 1,) + piece,
    ]
    dma = pltpu.SemaphoreType.DMA
    return pl.pallas_call(
        opening_kernel,
        in_specs=[anywhere] * 7,
        out_specs=[anywhere] * 13,
        out_shape=[jax.ShapeDtypeStruct(shape, BF) for shape in shapes],
        scratch_shapes=[
            dma((5, 8)),
            dma((5, 8)),
            dma((2, 8)),
            dma((2, 8)),
            dma((7,)),
            dma((4,)),
            dma((4,)),
            dma((8, n_a - 1)),
            dma((8, n_a - 1)),
        ],
        compiler_params=pltpu.CompilerParams(
            collective_id=1, has_side_effects=True, vmem_limit_bytes=8 * 2**20
        ),
        cost_estimate=pl.CostEstimate(flops=0, bytes_accessed=300 * 2**20, transcendentals=0),
    )(packed, grad_out, qkv_local, gain_tile, gate, up, down)


def norm_parts(value):
    return lax.rsqrt(jnp.mean(value * value, axis=-1, keepdims=True) + EPS)


def norm_back(value, gain, grad):
    r = norm_parts(value)
    hat = value * r
    scaled = grad * gain
    return r * (scaled - hat * jnp.mean(scaled * hat, axis=-1, keepdims=True)), hat


def local(
    inputs,
    lengths,
    positions,
    attn_gain,
    w_query,
    w_key,
    w_value,
    w_output,
    ffn_gain,
    w_gate,
    w_up,
    w_down,
    out_grad,
):
    _, slots, width = inputs.shape
    rows = w_gate.shape[0]
    h, l = lax.axis_index("h"), lax.axis_index("l")
    half = 2 * slots
    q_width = SHARE * SIZE
    own_slot = (h * 2 + l) * slots + jnp.arange(slots, dtype=jnp.int32)
    valid = (own_slot < lengths[0])[:, None]
    own = inputs[0]
    grad_out = jnp.where(valid, out_grad[0], jnp.zeros((), BF))

    numbers = jnp.stack([positions[0], jnp.broadcast_to(lengths, (slots,))], axis=-1)
    digits = jnp.concatenate([numbers // 128, numbers % 128], axis=-1).astype(BF)
    packed = jnp.concatenate([own, jnp.pad(digits, ((0, 0), (0, 124)))], axis=-1)
    gain_tile = jnp.pad(jnp.stack([attn_gain, ffn_gain]), ((0, 0), (0, 64 - rows)))
    gain_tile = jnp.broadcast_to(gain_tile.reshape(1, 128), (16, 128))
    qkv_local = jnp.concatenate(
        [w.reshape(rows, 8, -1) for w in (w_query, w_key, w_value)], axis=-1
    ).reshape(rows, -1)
    (
        team_packed,
        team_grad,
        slab,
        gains,
        gate0,
        gate_h,
        gate_a,
        gate_far,
        up0,
        up_h,
        up_a,
        down0,
        down_a,
    ) = opening_call(packed, grad_out, qkv_local, gain_tile, w_gate, w_up, w_down)
    slab, w_output = together(slab, w_output)
    w_out = lax.all_gather(w_output, EVERY, axis=0, tiled=True)
    steps = range(1, lax.axis_size("a"))
    w_qkv = slab.reshape(width, V_END)
    gains = gains.reshape(-1, 16, 128)[:, 0].astype(F32)
    attn_gain_full = gains[:, :rows].reshape(1, width)
    ffn_gain_full = gains[:, 64 : 64 + rows].reshape(1, width)
    down_h = shift(down0, "h", 1)
    up_far = [shift(up_h, "a", s) for s in steps]

    tokens = 8 * slots
    digits = team_packed[:, :, width : width + 4].reshape(tokens, 4).astype(jnp.int32)
    cosine, sine = rope_lanes(*rope_tables(digits[:, 0] * 128 + digits[:, 2]))
    team_lengths = (digits[:, 1] * 128 + digits[:, 3])[::half]
    normed_attn, qkv = project_call(team_packed, attn_gain_full, w_qkv, cosine, sine)
    qkv = qkv.reshape(4, half, V_END)
    early = lax.ppermute(qkv[:, :, Q_END:], "h", [(0, 1)])
    late = h.astype(jnp.int32).reshape(1)
    attended = attention_call(
        forward_kernel, late, team_lengths, (qkv, early), [(q_width, BF)], 3 * 10**9
    )[0]
    attended, down_h = together(attended, down_h)
    down_far = [shift(down_h, "a", s) for s in steps]
    attended = lax.all_to_all(attended.reshape(8, slots, q_width), TEAM, 0, 0, tiled=True)
    attended = attended.transpose(1, 0, 2).reshape(slots, HEADS * SIZE)

    hidden = own.astype(F32) + dot(attended, w_out, NN)
    normed_ffn = (hidden * norm_parts(hidden) * ffn_gain_full).astype(BF)

    pieces = [gate0, gate_a, gate_h, gate_far]
    pieces += [up0, up_a, up_h, jnp.stack(up_far)]
    pieces += [down0, down_a, down_h, jnp.stack(down_far)]
    grad_nffn, down_part, gate_dw, up_dw, down_dw = ffn_call(normed_ffn, team_grad, pieces)
    gate_sum = fold_a(gate_dw, rows)

    grad_hidden, hat = norm_back(hidden, ffn_gain_full, grad_nffn)
    grad_hidden = grad_hidden + grad_out.astype(F32)
    ffn_gain_term = jnp.sum(grad_nffn * hat, axis=0)

    grad_branch = grad_hidden.astype(BF)
    grad_attended = dot(grad_branch, w_out, NT).astype(BF)
    grad_heads = lax.all_to_all(
        grad_attended.reshape(slots, 8, q_width).transpose(1, 0, 2), TEAM, 0, 0, tiled=True
    ).reshape(4, half, q_width)
    grad_heads, gate_sum, up_dw, down_part = together(grad_heads, gate_sum, up_dw, down_part)
    up_sum = fold_a(up_dw, rows)
    gate_sum = scatter_step(gate_sum, "h", 1)
    output_grad = rows_scatter(dot(attended, grad_branch, TN), rows)
    grad_own, grad_early = attention_call(
        backward_kernel,
        late,
        team_lengths,
        (qkv, early, grad_heads),
        [(V_END, F32), (2 * SIZE, BF)],
        8 * 10**9,
    )
    back = lax.ppermute(grad_early, "h", [(1, 0)])
    back, up_sum, down_dw, gate_sum = together(back, up_sum, down_dw, gate_sum)
    down_sum = fold_a(down_dw, rows)
    up_sum = scatter_step(up_sum, "h", 1)
    grad_qkv = unrotate_call(
        grad_own.reshape(tokens, V_END), back.reshape(tokens, 2 * SIZE), cosine, sine
    )
    partial = dot(grad_qkv, w_qkv, NT)
    grad_nattn = team_scatter(partial)
    grad_input, _ = norm_back(own.astype(F32), attn_gain_full, grad_nattn)
    input_grad = (grad_hidden + grad_input).astype(BF)
    attn_gain_term = jnp.sum(partial * normed_attn.astype(F32), axis=0) / attn_gain_full[0]
    extra = jnp.stack([attn_gain_term, ffn_gain_term], axis=-1)
    extra = jnp.pad(extra, ((0, 0), (0, 126)))
    slab = jnp.concatenate([dot(normed_attn, grad_qkv, TN), extra], axis=-1)
    qkv_grad = fold_team(scatter_step(fold_a(slab, rows), "h", 1), rows)
    gain_grads = jnp.sum(qkv_grad[:, :, V_END : V_END + 2], axis=1)
    down_out = relative_scatter(down_part.reshape(2, 2, 2, slots, width))
    output = jnp.where(valid, hidden + down_out, 0.0).astype(BF)
    down_sum = scatter_step(down_sum, "h", 1)
    gate_grad, up_grad, down_grad = (
        fold_team(x, rows).reshape(rows, -1) for x in (gate_sum, up_sum, down_sum)
    )
    return (
        output[None],
        input_grad[None],
        gain_grads[:, 0],
        qkv_grad[:, :, :Q_END].reshape(rows, -1),
        qkv_grad[:, :, Q_END:K_END].reshape(rows, -1),
        qkv_grad[:, :, K_END:V_END].reshape(rows, -1),
        output_grad,
        gain_grads[:, 1],
        gate_grad,
        up_grad,
        down_grad,
    )


def solution(mesh):
    n_dp, n_seq = mesh.shape["dp"], mesh.shape["seq"]
    fine = Mesh(mesh.devices.reshape(n_dp // 4, 2, 2, n_seq // 2, 2), EVERY)
    tokens = P(("a", "b", "c"), ("h", "l"), None)
    matrix = P(EVERY, None)
    vector = P(EVERY)
    placed = (
        tokens,
        P(("a", "b", "c")),
        P(("a", "b", "c"), ("h", "l")),
        vector,
        matrix,
        matrix,
        matrix,
        matrix,
        vector,
        matrix,
        matrix,
        matrix,
        tokens,
    )
    return jax.shard_map(
        local,
        mesh=fine,
        in_specs=placed,
        out_specs=(
            tokens, tokens, vector, matrix, matrix, matrix, matrix, vector, matrix, matrix, matrix
        ),
        check_vma=False,
    )
```

```python
import functools
import math

import jax
import jax.numpy as jnp
from jax import lax
from jax.experimental import pallas as pl
from jax.experimental.pallas import tpu as pltpu
from jax.sharding import Mesh
from jax.sharding import PartitionSpec as P

HEADS = 32
GROUPS = 8
SIZE = 64
SHARE = HEADS // GROUPS
EPS = 1e-05
TEAM = ("b", "c", "l")
EVERY = ("a", "b", "c", "h", "l")
BF = jnp.bfloat16
F32 = jnp.float32


def rope_tables(positions):
    index = jnp.arange(SIZE // 2, dtype=F32)
    frequency = 1.0 / 500000.0 ** (2.0 * index / SIZE)
    wavelength = 2.0 * math.pi / frequency
    blending = (8192.0 / wavelength - 1.0) / (4.0 - 1.0)
    middle = (1.0 - blending) * frequency / 32.0 + blending * frequency
    scaled = jnp.where(
        wavelength < 8192.0 / 4.0,
        frequency,
        jnp.where(wavelength > 8192.0, frequency / 32.0, middle),
    )
    angles = positions.astype(F32)[..., None] * scaled
    angles = jnp.concatenate([angles, angles], axis=-1)
    return jnp.cos(angles), jnp.sin(angles)


def rope_lanes(cosine, sine):
    signed = jnp.where(jnp.arange(SIZE) < SIZE // 2, -sine, sine)
    ones, zeros = jnp.ones_like(cosine), jnp.zeros_like(sine)
    return (
        jnp.concatenate([cosine, cosine, cosine, ones], axis=-1),
        jnp.concatenate([signed, signed, signed, zeros], axis=-1),
    )


def swap_halves(v):
    lane = lax.broadcasted_iota(jnp.int32, v.shape, 1)
    low = lax.rem(lane, SIZE) < SIZE // 2
    return jnp.where(low, pltpu.roll(v, 128 - SIZE // 2, 1), pltpu.roll(v, SIZE // 2, 1))


def rope_blocks(v, cosine, sine, sign):
    outs = []
    for n in range(3):
        block = v[:, n * 128 : (n + 1) * 128]
        cols = slice(128, 256) if n == 2 else slice(0, 128)
        outs.append(block * cosine[:, cols] + sign * swap_halves(block) * sine[:, cols])
    return jnp.concatenate(outs, axis=-1)


def shift(value, axis, step):
    n = lax.axis_size(axis)
    return lax.ppermute(value, axis, [(i, (i + step) % n) for i in range(n)])


def after(value, earlier):
    return lax.optimization_barrier((value, earlier))[0]


def scatter_step(value, axis, dim, pin=None):
    n = lax.axis_size(axis)
    me = lax.axis_index(axis)
    kept = lax.dynamic_index_in_dim(value, me, dim, keepdims=False).astype(F32)
    for s in range(1, n):
        sent = lax.dynamic_index_in_dim(value, lax.rem(me + s, n), dim, keepdims=False)
        arrived = shift(sent.astype(BF), axis, s)
        if pin is not None:
            arrived = after(arrived, pin)
        kept = kept + arrived.astype(F32)
    return kept


def team_scatter(partial):
    width = partial.shape[-1]
    view = partial.reshape(2, 2, 2, -1, width)
    view = scatter_step(view, "c", 1)
    left = scatter_step(view[..., : width // 2], "l", 1)
    left = scatter_step(left, "b", 0)
    right = scatter_step(view[..., width // 2 :], "b", 0)
    right = scatter_step(right, "l", 0)
    return jnp.concatenate([left, right], axis=-1)


def together(*values):
    return lax.optimization_barrier(values)


def fold_a(partial, rows, pin=None):
    view = partial.reshape(lax.axis_size("a"), 4, lax.axis_size("h"), 2 * rows, partial.shape[-1])
    return scatter_step(view, "a", 0, pin)


def fold_team(view, rows):
    owned = lax.all_to_all(
        view.reshape(8, rows, view.shape[-1]).astype(BF), TEAM, 0, 0, tiled=True
    )
    return owned.transpose(1, 0, 2).astype(F32)


def fold(value, axis, dim, pin=None):
    kept = lax.index_in_dim(value, 0, dim, keepdims=False).astype(F32)
    sent = lax.index_in_dim(value, 1, dim, keepdims=False).astype(BF)
    arrived = shift(sent, axis, 1)
    if pin is not None:
        arrived = after(arrived, pin)
    return kept + arrived.astype(F32)


def dot(a, b, over):
    return lax.dot_general(a, b, ((over[0], over[1]), ((), ())), preferred_element_type=F32)


NN = ((1,), (0,))
NT = ((1,), (1,))
TN = ((0,), (0,))


def softmax_parts(late, length, q, keys, early_keys):
    rows = q.shape[0]
    slot = late * rows + lax.broadcasted_iota(jnp.int32, (rows, rows), 0)
    key_slot = late * rows + lax.broadcasted_iota(jnp.int32, (rows, rows), 1)
    allowed = (key_slot <= slot) & (key_slot < length)
    own = jnp.where(allowed, dot(q, keys, NT) * SIZE**-0.5, -1e30)
    early_slot = lax.broadcasted_iota(jnp.int32, (rows, rows), 1)
    early = jnp.where(
        (early_slot < late * rows) & (early_slot < length), dot(q, early_keys, NT) * SIZE**-0.5, -1e30
    )
    peak = jnp.maximum(
        jnp.max(own, axis=-1, keepdims=True), jnp.max(early, axis=-1, keepdims=True)
    )
    own, early = jnp.exp(own - peak), jnp.exp(early - peak)
    total = jnp.sum(own, axis=-1, keepdims=True) + jnp.sum(early, axis=-1, keepdims=True)
    part = 1.0 / total
    return own * part, early * part


Q_END, K_END, V_END = SHARE * SIZE, SHARE * SIZE + SIZE, SHARE * SIZE + 2 * SIZE


def project_kernel(x_ref, gain_ref, w_ref, cos_ref, sin_ref, normed_ref, out_ref):
    x = x_ref[0].astype(F32)
    normed = (x * norm_parts(x) * gain_ref[...]).astype(BF)
    normed_ref[...] = normed
    qkv = dot(normed, w_ref[...], NN)
    out_ref[...] = rope_blocks(qkv, cos_ref[...], sin_ref[...], 1.0).astype(BF)


def project_call(team_packed, gain, w_qkv, cosine, sine):
    _, rows, _ = team_packed.shape
    width = gain.shape[-1]
    return pl.pallas_call(
        project_kernel,
        grid=(8,),
        in_specs=[
            pl.BlockSpec((1, rows, width), lambda i: (i, 0, 0)),
            pl.BlockSpec((1, width), lambda i: (0, 0)),
            pl.BlockSpec((width, V_END), lambda i: (0, 0)),
            pl.BlockSpec((rows, 256), lambda i: (i, 0)),
            pl.BlockSpec((rows, 256), lambda i: (i, 0)),
        ],
        out_specs=[
            pl.BlockSpec((rows, width), lambda i: (i, 0)),
            pl.BlockSpec((rows, V_END), lambda i: (i, 0)),
        ],
        out_shape=[
            jax.ShapeDtypeStruct((8 * rows, width), BF),
            jax.ShapeDtypeStruct((8 * rows, V_END), BF),
        ],
        compiler_params=pltpu.CompilerParams(vmem_limit_bytes=40 * 2**20),
        cost_estimate=pl.CostEstimate(
            flops=16 * rows * width * V_END, bytes_accessed=24 * 2**20, transcendentals=0
        ),
    )(team_packed, gain, w_qkv, cosine, sine)


def unrotate_kernel(own_ref, back_ref, cos_ref, sin_ref, out_ref):
    own = own_ref[...]
    tail = own[:, Q_END:] + back_ref[...].astype(F32)
    total = jnp.concatenate([own[:, :Q_END], tail], axis=-1)
    out_ref[...] = rope_blocks(total, cos_ref[...], sin_ref[...], -1.0).astype(BF)


def unrotate_call(own, back, cosine, sine):
    tokens = own.shape[0]
    rows = tokens // 4

    def spec(x):
        return pl.BlockSpec((rows, x.shape[1]), lambda i: (i, 0))

    return pl.pallas_call(
        unrotate_kernel,
        grid=(4,),
        in_specs=[spec(x) for x in (own, back, cosine, sine)],
        out_specs=spec(own),
        out_shape=jax.ShapeDtypeStruct(own.shape, BF),
        cost_estimate=pl.CostEstimate(flops=10**7, bytes_accessed=9 * 2**20, transcendentals=0),
    )(own, back, cosine, sine)


def forward_kernel(late_ref, length_ref, qkv_ref, early_ref, o_ref):
    late, length = late_ref[0], length_ref[pl.program_id(0)]
    keys, values = qkv_ref[0, :, Q_END:K_END], qkv_ref[0, :, K_END:V_END]
    early_keys, early_values = early_ref[0, :, :SIZE], early_ref[0, :, SIZE:]
    outs = []
    for head in range(SHARE):
        q = qkv_ref[0, :, head * SIZE : (head + 1) * SIZE]
        own, early = softmax_parts(late, length, q, keys, early_keys)
        outs.append(dot(own.astype(BF), values, NN) + dot(early.astype(BF), early_values, NN))
    o_ref[0] = jnp.concatenate(outs, axis=-1).astype(BF)


def backward_kernel(late_ref, length_ref, qkv_ref, early_ref, g_ref, d_ref, ed_ref):
    late, length = late_ref[0], length_ref[pl.program_id(0)]
    keys, values = qkv_ref[0, :, Q_END:K_END], qkv_ref[0, :, K_END:V_END]
    early_keys, early_values = early_ref[0, :, :SIZE], early_ref[0, :, SIZE:]
    scale = SIZE**-0.5
    dqs = []
    dk = dv = edk = edv = 0.0
    for head in range(SHARE):
        q = qkv_ref[0, :, head * SIZE : (head + 1) * SIZE]
        g = g_ref[0, :, head * SIZE : (head + 1) * SIZE]
        own, early = softmax_parts(late, length, q, keys, early_keys)
        dp, edp = dot(g, values, NT), dot(g, early_values, NT)
        inner = jnp.sum(own * dp, axis=-1, keepdims=True) + jnp.sum(
            early * edp, axis=-1, keepdims=True
        )
        ds = (own * (dp - inner)).astype(BF)
        eds = (early * (edp - inner)).astype(BF)
        dqs.append((dot(ds, keys, NN) + dot(eds, early_keys, NN)) * scale)
        dv = dv + dot(own.astype(BF), g, TN)
        edv = edv + dot(early.astype(BF), g, TN)
        dk = dk + dot(ds, q, TN)
        edk = edk + dot(eds, q, TN)
    d_ref[0] = jnp.concatenate(dqs + [dk * scale, dv], axis=-1)
    ed_ref[0] = jnp.concatenate([edk * scale, edv], axis=-1).astype(BF)


def attention_call(kernel, late, lengths, arrays, outs, flops):
    count, rows, _ = arrays[0].shape

    def spec(width):
        return pl.BlockSpec((1, rows, width), lambda s, *_: (s, 0, 0))

    return pl.pallas_call(
        kernel,
        grid_spec=pltpu.PrefetchScalarGridSpec(
            num_scalar_prefetch=2,
            grid=(count,),
            in_specs=[spec(x.shape[-1]) for x in arrays],
            out_specs=[spec(width) for width, _ in outs],
        ),
        out_shape=[jax.ShapeDtypeStruct((count, rows, width), kind) for width, kind in outs],
        compiler_params=pltpu.CompilerParams(vmem_limit_bytes=48 * 2**20),
        cost_estimate=pl.CostEstimate(flops=flops, bytes_accessed=8 * 2**20, transcendentals=2**23),
    )(late, lengths, *arrays)


MESH = pl.DeviceIdType.MESH


def ffn_kernel(
    own_ref,
    grad_ref,
    *refs,
):
    n_pieces = len(refs) - 28
    ffn_body(own_ref, grad_ref, refs[:n_pieces], *refs[n_pieces:])


def ffn_body(
    own_ref,
    grad_ref,
    piece_refs,
    gn_ref,
    dn_ref,
    dwg_ref,
    dwu_ref,
    dwd_ref,
    wg,
    wu,
    wd,
    xs,
    gs,
    act,
    gg,
    gu,
    send_sib,
    recv_sib,
    send_own,
    recv_own,
    stage,
    local_sem,
    grad_sem,
    ag_send,
    ag_recv,
    sib_send,
    sib_recv,
    own_send,
    own_recv,
    stage_sem,
    credit,
):
    b, c, l = lax.axis_index("b"), lax.axis_index("c"), lax.axis_index("l")
    rows, width = own_ref.shape
    tile = wg.shape[1]
    sibling = {"c": 1 - c}

    def chip(k):
        return {"b": lax.rem(b + lax.rem(k, 2), 2), "l": lax.rem(l + k // 2, 2)}

    barrier = pltpu.get_barrier_semaphore()
    for peer in (sibling, chip(1), chip(2), chip(3)):
        pl.semaphore_signal(barrier, inc=1, device_id=peer, device_id_type=MESH)
    pl.semaphore_wait(barrier, 4)

    def part(slot):
        return pl.ds(pl.multiple_of(slot * rows, rows), rows)

    def gather_copy(source, slot, peer):
        return pltpu.make_async_remote_copy(
            src_ref=source,
            dst_ref=xs.at[part(slot)],
            send_sem=ag_send.at[slot],
            recv_sem=ag_recv.at[slot],
            device_id=peer,
            device_id_type=MESH,
        )

    def forward_copy(k):
        return gather_copy(xs.at[part(2 * k)], 2 * k + 1, sibling)

    def sibling_copy(k):
        spot = lax.rem(k, 2)
        return pltpu.make_async_remote_copy(
            src_ref=send_sib.at[spot],
            dst_ref=recv_sib.at[spot],
            send_sem=sib_send.at[spot],
            recv_sem=sib_recv.at[spot],
            device_id=sibling,
            device_id_type=MESH,
        )

    def owner_copy(k):
        return pltpu.make_async_remote_copy(
            src_ref=send_own.at[k - 1],
            dst_ref=recv_own.at[k - 1],
            send_sem=own_send.at[k - 1],
            recv_sem=own_recv.at[k - 1],
            device_id=chip(k),
            device_id_type=MESH,
        )

    def grad_copy(slot):
        k, dc = slot // 2, lax.rem(slot, 2)
        db, dl = lax.rem(k, 2), k // 2
        source = (lax.rem(b + db, 2) * 2 + lax.rem(c + dc, 2)) * 2 + lax.rem(l + dl, 2)
        return pltpu.make_async_copy(grad_ref.at[source], gs.at[part(slot)], grad_sem.at[slot])

    def down_copy(spot, slot):
        cols = pl.ds(spot * tile, tile)
        return pltpu.make_async_copy(stage.at[spot], dn_ref.at[slot, :, cols], stage_sem.at[spot])

    gather_copy(own_ref, 1, sibling).start()
    for k in (1, 2, 3):
        gather_copy(own_ref, 2 * k, chip(k)).start()
    own_copy = pltpu.make_async_copy(own_ref, xs.at[part(0)], local_sem.at[0])
    own_copy.start()
    a, h = lax.axis_index("a"), lax.axis_index("h")
    n_a, n_h = lax.axis_size("a"), lax.axis_size("h")
    chunk = piece_refs[0].shape[1]
    for j, target in enumerate((wg, wu, wd)):
        near, near_a, far, far_a = piece_refs[4 * j : 4 * j + 4]
        for dh, first, rest in ((0, near, near_a), (1, far, far_a)):
            for da in range(n_a):
                source = rest.at[da - 1] if da else first
                ra, rh = lax.rem(a + n_a - da, n_a), lax.rem(h + dh, n_h)
                for pair in range(4):
                    start = pl.multiple_of(((ra * 4 + pair) * n_h + rh) * chunk, chunk)
                    pltpu.make_async_copy(
                        source.at[pair], target.at[pl.ds(start, chunk)], local_sem.at[1 + j]
                    ).start()
    for slot in range(8):
        grad_copy(slot).start()
    for j, target in enumerate((wg, wu, wd)):
        pltpu.make_async_copy(target, target, local_sem.at[1 + j]).wait()
    own_copy.wait()

    def block(i, carry):
        k, second = i // 2, lax.rem(i, 2)
        slot = 2 * k + 1 - second
        spot = lax.rem(k, 2)
        for at, ready in ((2, 1), (3, 2), (5, 3)):

            @pl.when(i == at)
            def _():
                gather_copy(own_ref, 2 * ready, chip(ready)).wait_recv()
                forward_copy(ready).start()

        @pl.when(second == 0)
        def _():
            gather_copy(own_ref, slot, sibling).wait_recv()

        grad_copy(slot).wait()
        for piece in (slice(0, tile // 2), slice(tile // 2, tile)):
            gate = dot(xs[part(slot), :], wg[:, piece], NN)
            up = dot(xs[part(slot), :], wu[:, piece], NN)
            grad_act = dot(gs[part(slot), :], wd[:, piece], NN)
            sigmoid = jax.nn.sigmoid(gate)
            silu = gate * sigmoid
            act[part(slot), piece] = (silu * up).astype(BF)
            gu[part(slot), piece] = (grad_act * silu).astype(BF)
            slope = sigmoid * (1.0 + gate * (1.0 - sigmoid))
            gg[part(slot), piece] = (grad_act * up * slope).astype(BF)

        @pl.when((second == 0) & (k >= 2))
        def _():
            sibling_copy(k).wait_send()

        @pl.when(second == 1)
        def _():
            sibling_copy(k).wait_recv()

        for start in range(0, width, tile):
            cols = slice(start, start + tile)
            part_gn = dot(gg[part(slot), :], wg[cols, :], NT)
            part_gn += dot(gu[part(slot), :], wu[cols, :], NT)

            @pl.when(second == 0)
            def _():
                send_sib[spot, :, cols] = part_gn.astype(BF)

            @pl.when(i == 1)
            def _():
                gn_ref[:, cols] = part_gn + recv_sib[spot, :, cols].astype(F32)

            @pl.when((second == 1) & (k > 0))
            def _():
                send_own[k - 1, :, cols] = (part_gn + recv_sib[spot, :, cols].astype(F32)).astype(BF)

        @pl.when((second == 0) & (k >= 2))
        def _():
            pl.semaphore_wait(credit, 1)

        @pl.when(second == 0)
        def _():
            sibling_copy(k).start()

        @pl.when((second == 1) & (k < 2))
        def _():
            pl.semaphore_signal(credit, inc=1, device_id=sibling, device_id_type=MESH)

        @pl.when((second == 1) & (k > 0))
        def _():
            owner_copy(k).start()

        for at in range(width // tile):
            part_dn = dot(act[part(slot), :], wd[at * tile : (at + 1) * tile, :], NT)

            @pl.when(i >= 1)
            def _():
                down_copy(at, slot).wait()

            stage[at] = part_dn.astype(BF)
            down_copy(at, slot).start()
        return carry

    lax.fori_loop(0, 8, block, 0)
    for at in range(width // tile):
        down_copy(at, 0).wait()

    step = rows

    def weight_copy(j, which, target):
        return pltpu.make_async_copy(
            stage.at[which],
            target.at[pl.ds(pl.multiple_of(j * step, step), step)],
            stage_sem.at[which],
        )

    def weights(j, carry):
        cols = pl.ds(pl.multiple_of(j * step, step), step)
        for which, (left, right, target) in enumerate(
            ((xs, gg, dwg_ref), (xs, gu, dwu_ref), (gs, act, dwd_ref))
        ):

            @pl.when(j > 0)
            def _():
                weight_copy(j, which, target).wait()

            stage[which] = dot(left[:, cols], right[...], TN).astype(BF)
            weight_copy(j, which, target).start()
        return carry

    lax.fori_loop(0, width // step, weights, 0)

    for k in (1, 2, 3):
        owner_copy(k).wait_recv()
        gn_ref[...] += recv_own[k - 1].astype(F32)
    for which, target in enumerate((dwg_ref, dwu_ref, dwd_ref)):
        weight_copy(0, which, target).wait()
    for k in (0, 1):
        sibling_copy(k).wait_send()
    gather_copy(own_ref, 1, sibling).wait_send()
    for k in (1, 2, 3):
        gather_copy(own_ref, 2 * k, chip(k)).wait_send()
        forward_copy(k).wait_send()
        owner_copy(k).wait_send()


def ffn_call(own, team_grad, pieces):
    rows, width = own.shape
    hidden = pieces[0].shape[-1]
    team = 8 * rows
    anywhere = pl.BlockSpec(memory_space=pl.ANY)
    stages = max(3, width // hidden)
    return pl.pallas_call(
        ffn_kernel,
        in_specs=[anywhere] * (2 + len(pieces)),
        out_specs=[pl.BlockSpec(memory_space=pltpu.VMEM)] + [anywhere] * 4,
        out_shape=[
            jax.ShapeDtypeStruct((rows, width), F32),
            jax.ShapeDtypeStruct((8, rows, width), BF),
        ]
        + [jax.ShapeDtypeStruct((width, hidden), BF)] * 3,
        scratch_shapes=[pltpu.VMEM((width, hidden), BF)] * 3
        + [pltpu.VMEM((team, width), BF)] * 2
        + [pltpu.VMEM((team, hidden), BF)] * 3
        + [pltpu.VMEM((2, rows, width), BF)] * 2
        + [pltpu.VMEM((3, rows, width), BF)] * 2
        + [pltpu.VMEM((stages, rows, hidden), BF)]
        + [pltpu.SemaphoreType.DMA((n,)) for n in (4, 8, 8, 8, 2, 2, 3, 3, stages)]
        + [pltpu.SemaphoreType.REGULAR],
        compiler_params=pltpu.CompilerParams(
            collective_id=0, has_side_effects=True, vmem_limit_bytes=60 * 2**20
        ),
        cost_estimate=pl.CostEstimate(
            flops=18 * team * width * hidden, bytes_accessed=60 * 2**20, transcendentals=team * hidden
        ),
    )(own, team_grad, *pieces)


def opening_kernel(
    tok_ref,
    grad_ref,
    qkv_ref,
    gain_ref,
    gate_ref,
    up_ref,
    down_ref,
    toks,
    grads,
    slab,
    gains,
    gate0,
    gate_h,
    gate_a,
    gate_far,
    up0,
    up_h,
    up_a,
    down0,
    down_a,
    team_send,
    team_recv,
    tok_send,
    tok_recv,
    local_sem,
    h_send,
    h_recv,
    a_send,
    a_recv,
):
    a, b, c, h, l = (lax.axis_index(axis) for axis in EVERY)
    n_a = lax.axis_size("a")
    n_rows = qkv_ref.shape[0]
    q_wide, f_wide, g_rows = slab.shape[-1], gate0.shape[-1], gain_ref.shape[0]

    def flip(off):
        return lax.rem(b + off // 4, 2), lax.rem(c + off // 2 % 2, 2), lax.rem(l + off % 2, 2)

    def peer(off):
        pb, pc, p_l = flip(off)
        return {"b": pb, "c": pc, "l": p_l}

    def number(off):
        pb, pc, p_l = flip(off)
        return (pb * 2 + pc) * 2 + p_l

    def a_peer(step):
        return {"a": lax.rem(a + step, n_a)}

    h_peer = {"h": 1 - h}
    barrier = pltpu.get_barrier_semaphore()
    others = [peer(off) for off in range(1, 8)] + [h_peer] + [a_peer(s) for s in range(1, n_a)]
    for other in others:
        pl.semaphore_signal(barrier, inc=1, device_id=other, device_id_type=MESH)
    pl.semaphore_wait(barrier, len(others))

    def source(which, off):
        t = number(off)
        if which == 0:
            return qkv_ref.at[:, pl.ds(pl.multiple_of(t * q_wide, 128), q_wide)]
        if which == 1:
            return gain_ref
        ref = (gate_ref, up_ref, down_ref)[which - 2]
        return ref.at[:, pl.ds(pl.multiple_of(t * f_wide, 128), f_wide)]

    def place(which, off):
        pb, pc, p_l = flip(off)
        pair = pb * 2 + pc
        rows = pl.ds(pl.multiple_of(p_l * n_rows, n_rows), n_rows)
        if which == 0:
            return slab.at[a, pair, h, rows]
        if which == 1:
            return gains.at[a, pair, h, pl.ds(pl.multiple_of(p_l * g_rows, g_rows), g_rows)]
        return (gate0, up0, down0)[which - 2].at[pair, rows]

    def team_copy(which, off, arriving=False):
        return pltpu.make_async_remote_copy(
            src_ref=source(which, off),
            dst_ref=place(which, off if arriving else 0),
            send_sem=team_send.at[which, off],
            recv_sem=team_recv.at[which, off],
            device_id=peer(off),
            device_id_type=MESH,
        )

    def own_copy(which):
        return pltpu.make_async_copy(source(which, 0), place(which, 0), local_sem.at[which])

    def tok_copy(which, from_off, to_off, sem):
        whole = (toks, grads)[which]
        held = (tok_ref, grad_ref)[which] if sem < 6 and sem != 3 else whole.at[number(from_off)]
        return pltpu.make_async_remote_copy(
            src_ref=held,
            dst_ref=whole.at[number(from_off)],
            send_sem=tok_send.at[which, sem],
            recv_sem=tok_recv.at[which, sem],
            device_id=peer(to_off),
            device_id_type=MESH,
        )

    def forward(which, off):
        return tok_copy(which, off, 2, off + 2)

    def diagonal(which, half, arriving=False):
        whole = (toks, grads)[which]
        rows = whole.shape[1] // 2
        owner, to, sem = ((4, 1, 5), (1, 4, 0))[half]
        spot = pl.ds(half * rows, rows)
        return pltpu.make_async_remote_copy(
            src_ref=whole.at[number(owner), spot],
            dst_ref=whole.at[number(5 if arriving else owner), spot],
            send_sem=tok_send.at[which, sem],
            recv_sem=tok_recv.at[which, sem],
            device_id=peer(to),
            device_id_type=MESH,
        )

    def hand_on(which):
        for half, off in enumerate((4, 1)):
            tok_copy(which, off, off, off).wait_recv()
            diagonal(which, half).start()
            forward(which, off).start()

    def diagonal_arrived(which):
        for half in (0, 1):
            diagonal(which, half, arriving=True).wait_recv()
        forward(which, 5).start()

    def region(which, ra, rh):
        if which == 0:
            return slab.at[ra, :, rh]
        return gains.at[ra, :, rh]

    def h_copy(which, arriving=False):
        if which >= 2:
            src, dst = ((gate0, gate_h), (up0, up_h))[which - 2]
        else:
            src = region(which, a, h)
            dst = region(which, a, 1 - h if arriving else h)
        return pltpu.make_async_remote_copy(
            src_ref=src,
            dst_ref=dst,
            send_sem=h_send.at[which],
            recv_sem=h_recv.at[which],
            device_id=h_peer,
            device_id_type=MESH,
        )

    def a_copy(which, step, arriving=False):
        if which >= 4:
            src = (gate0, up0, down0, gate_h)[which - 4]
            dst = (gate_a, up_a, down_a, gate_far)[which - 4].at[step - 1]
        else:
            rh = h if which < 2 else 1 - h
            src = region(which % 2, a, rh)
            dst = region(which % 2, lax.rem(a + n_a - step, n_a) if arriving else a, rh)
        return pltpu.make_async_remote_copy(
            src_ref=src,
            dst_ref=dst,
            send_sem=a_send.at[which, step - 1],
            recv_sem=a_recv.at[which, step - 1],
            device_id=a_peer(step),
            device_id_type=MESH,
        )

    def team_arrived(which):
        own_copy(which).wait()
        for off in range(1, 8):
            team_copy(which, off, arriving=True).wait_recv()

    away = (4, 1, 5)
    steps = range(1, n_a)

    def team_start(*which):
        for w in which:
            for off in range(1, 8):
                team_copy(w, off).start()
            own_copy(w).start()

    def a_start(*which):
        for w in which:
            for step in steps:
                a_copy(w, step).start()

    team_start(0, 1)
    own_toks = [
        pltpu.make_async_copy(src, dst.at[number(0)], local_sem.at[5 + n])
        for n, (src, dst) in enumerate(((tok_ref, toks), (grad_ref, grads)))
    ]
    for which in (0, 1):
        own_toks[which].start()
        tok_copy(which, 0, 2, 2).start()
    team_arrived(0)
    team_arrived(1)
    h_copy(0).start()
    h_copy(1).start()
    a_start(0, 1)
    team_start(2, 3)
    team_arrived(2)
    a_start(4)
    for off in (4, 1):
        tok_copy(0, 0, off, off).start()
    team_arrived(3)
    a_start(5)
    team_start(4)
    for which in (0, 1):
        h_copy(which, arriving=True).wait_recv()
    h_copy(2).start()
    a_start(2, 3)
    hand_on(0)
    for off in (4, 1):
        tok_copy(1, 0, off, off).start()
    diagonal_arrived(0)
    team_arrived(4)
    a_start(6)
    h_copy(2).wait_recv()
    h_copy(3).start()
    a_start(7)
    hand_on(1)
    diagonal_arrived(1)
    for which in (0, 1):
        own_toks[which].wait()
        tok_copy(which, 2, 2, 2).wait_recv()
        for off in away:
            tok_copy(which, off + 2, 2, off + 2).wait_recv()
    for which in range(8):
        for step in steps:
            a_copy(which, step, arriving=True).wait_recv()
            a_copy(which, step).wait_send()
    h_copy(3).wait_recv()
    for which in range(4):
        h_copy(which).wait_send()
    for which in range(5):
        for off in range(1, 8):
            team_copy(which, off).wait_send()
    for which in (0, 1):
        for off in (2, 4, 1):
            tok_copy(which, 0, off, off).wait_send()
        for half in (0, 1):
            diagonal(which, half).wait_send()
        for off in away:
            forward(which, off).wait_send()


def opening_call(packed, grad_out, qkv_local, gain_tile, gate, up, down):
    n_a, n_h = lax.axis_size("a"), lax.axis_size("h")
    rows = gate.shape[0]
    q_wide, f_wide = qkv_local.shape[1] // 8, gate.shape[1] // 8
    anywhere = pl.BlockSpec(memory_space=pl.ANY)
    piece = (4, 2 * rows, f_wide)
    shapes = [
        (8,) + packed.shape,
        (8,) + grad_out.shape,
        (n_a, 4, n_h, 2 * rows, q_wide),
        (n_a, 4, n_h, 2 * gain_tile.shape[0], 128),
        piece,
        piece,
        (n_a - 1,) + piece,
        (n_a - 1,) + piece,
        piece,
        piece,
        (n_a - 1,) + piece,
        piece,
        (n_a - 1,) + piece,
    ]
    dma = pltpu.SemaphoreType.DMA
    return pl.pallas_call(
        opening_kernel,
        in_specs=[anywhere] * 7,
        out_specs=[anywhere] * 13,
        out_shape=[jax.ShapeDtypeStruct(shape, BF) for shape in shapes],
        scratch_shapes=[
            dma((5, 8)),
            dma((5, 8)),
            dma((2, 8)),
            dma((2, 8)),
            dma((7,)),
            dma((4,)),
            dma((4,)),
            dma((8, n_a - 1)),
            dma((8, n_a - 1)),
        ],
        compiler_params=pltpu.CompilerParams(
            collective_id=1, has_side_effects=True, vmem_limit_bytes=8 * 2**20
        ),
        cost_estimate=pl.CostEstimate(flops=0, bytes_accessed=300 * 2**20, transcendentals=0),
    )(packed, grad_out, qkv_local, gain_tile, gate, up, down)


def norm_parts(value):
    return lax.rsqrt(jnp.mean(value * value, axis=-1, keepdims=True) + EPS)


def norm_back(value, gain, grad):
    r = norm_parts(value)
    hat = value * r
    scaled = grad * gain
    return r * (scaled - hat * jnp.mean(scaled * hat, axis=-1, keepdims=True)), hat


def local(
    inputs,
    lengths,
    positions,
    attn_gain,
    w_query,
    w_key,
    w_value,
    w_output,
    ffn_gain,
    w_gate,
    w_up,
    w_down,
    out_grad,
):
    _, slots, width = inputs.shape
    rows = w_gate.shape[0]
    h, l = lax.axis_index("h"), lax.axis_index("l")
    half = 2 * slots
    q_width = SHARE * SIZE
    own_slot = (h * 2 + l) * slots + jnp.arange(slots, dtype=jnp.int32)
    valid = (own_slot < lengths[0])[:, None]
    own = inputs[0]
    grad_out = jnp.where(valid, out_grad[0], jnp.zeros((), BF))

    numbers = jnp.stack([positions[0], jnp.broadcast_to(lengths, (slots,))], axis=-1)
    digits = jnp.concatenate([numbers // 128, numbers % 128], axis=-1).astype(BF)
    packed = jnp.concatenate([own, jnp.pad(digits, ((0, 0), (0, 124)))], axis=-1)
    gain_tile = jnp.pad(jnp.stack([attn_gain, ffn_gain]), ((0, 0), (0, 64 - rows)))
    gain_tile = jnp.broadcast_to(gain_tile.reshape(1, 128), (16, 128))
    qkv_local = jnp.concatenate(
        [w.reshape(rows, 8, -1) for w in (w_query, w_key, w_value)], axis=-1
    ).reshape(rows, -1)
    (
        team_packed,
        team_grad,
        slab,
        gains,
        gate0,
        gate_h,
        gate_a,
        gate_far,
        up0,
        up_h,
        up_a,
        down0,
        down_a,
    ) = opening_call(packed, grad_out, qkv_local, gain_tile, w_gate, w_up, w_down)
    slab, w_output = together(slab, w_output)
    w_out = lax.all_gather(w_output, EVERY, axis=0, tiled=True)
    steps = range(1, lax.axis_size("a"))
    w_qkv = slab.reshape(width, V_END)
    gains = gains.reshape(-1, 16, 128)[:, 0].astype(F32)
    attn_gain_full = gains[:, :rows].reshape(1, width)
    ffn_gain_full = gains[:, 64 : 64 + rows].reshape(1, width)
    down_h = shift(down0, "h", 1)
    up_far = [shift(up_h, "a", s) for s in steps]

    tokens = 8 * slots
    digits = team_packed[:, :, width : width + 4].reshape(tokens, 4).astype(jnp.int32)
    cosine, sine = rope_lanes(*rope_tables(digits[:, 0] * 128 + digits[:, 2]))
    team_lengths = (digits[:, 1] * 128 + digits[:, 3])[::half]
    normed_attn, qkv = project_call(team_packed, attn_gain_full, w_qkv, cosine, sine)
    qkv = qkv.reshape(4, half, V_END)
    early = lax.ppermute(qkv[:, :, Q_END:], "h", [(0, 1)])
    late = h.astype(jnp.int32).reshape(1)
    attended = attention_call(
        forward_kernel, late, team_lengths, (qkv, early), [(q_width, BF)], 3 * 10**9
    )[0]
    attended, down_h = together(attended, down_h)
    down_far = [shift(down_h, "a", s) for s in steps]
    attended = lax.all_to_all(attended.reshape(8, slots, q_width), TEAM, 0, 0, tiled=True)
    attended = attended.transpose(1, 0, 2).reshape(slots, HEADS * SIZE)

    hidden = own.astype(F32) + dot(attended, w_out, NN)
    normed_ffn = (hidden * norm_parts(hidden) * ffn_gain_full).astype(BF)

    pieces = [gate0, gate_a, gate_h, gate_far]
    pieces += [up0, up_a, up_h, jnp.stack(up_far)]
    pieces += [down0, down_a, down_h, jnp.stack(down_far)]
    grad_nffn, down_part, gate_dw, up_dw, down_dw = ffn_call(normed_ffn, team_grad, pieces)
    down_view = down_part.reshape(2, 2, 2, slots, width)

    grad_hidden, hat = norm_back(hidden, ffn_gain_full, grad_nffn)
    grad_hidden = grad_hidden + grad_out.astype(F32)
    ffn_gain_term = jnp.sum(grad_nffn * hat, axis=0)

    grad_branch = grad_hidden.astype(BF)
    grad_attended = dot(grad_branch, w_out, NT).astype(BF)
    grad_heads = lax.all_to_all(
        grad_attended.reshape(slots, 8, q_width).transpose(1, 0, 2), TEAM, 0, 0, tiled=True
    ).reshape(4, half, q_width)
    down_view = fold(down_view, "c", 2)
    output_part = dot(attended, grad_branch, TN).astype(BF)
    grad_heads, down_view, output_part = together(grad_heads, down_view, output_part)
    grad_own, grad_early = attention_call(
        backward_kernel,
        late,
        team_lengths,
        (qkv, early, grad_heads),
        [(V_END, F32), (2 * SIZE, BF)],
        8 * 10**9,
    )
    down_left = fold(down_view[..., : width // 2], "l", 0, grad_own)
    down_right = fold(down_view[..., width // 2 :], "b", 1, grad_own)
    gate_sum = fold_a(gate_dw, rows, grad_own)
    back = lax.ppermute(grad_early, "h", [(1, 0)])
    grad_qkv = unrotate_call(
        grad_own.reshape(tokens, V_END), back.reshape(tokens, 2 * SIZE), cosine, sine
    )
    n_a, n_h = lax.axis_size("a"), lax.axis_size("h")
    output_view = output_part.reshape(n_a, 2, 2, n_h, 2, rows, -1)
    output_view = scatter_step(output_view, "c", 2, grad_own)
    gate_sum = scatter_step(after(gate_sum, back), "h", 1, grad_qkv)
    up_sum = fold_a(up_dw, rows, grad_qkv)
    partial = dot(grad_qkv, w_qkv, NT)
    partial_view = scatter_step(partial.reshape(2, 2, 2, slots, width), "c", 1)
    attn_gain_term = jnp.sum(partial * normed_attn.astype(F32), axis=0) / attn_gain_full[0]
    terms = jnp.pad(jnp.stack([attn_gain_term, ffn_gain_term]), ((0, 6), (0, 0)))
    extra = lax.dot_general(
        terms, jnp.eye(8, 128, dtype=F32), ((TN[0], TN[1]), ((), ())), precision=lax.Precision.HIGHEST
    )
    slab = jnp.concatenate([dot(normed_attn, grad_qkv, TN), extra], axis=-1).astype(BF)
    slab, partial_view, up_sum = together(slab, partial_view, up_sum)
    left = scatter_step(partial_view[..., : width // 2], "l", 1, slab)
    right = scatter_step(partial_view[..., width // 2 :], "b", 0, slab)
    down_left = fold(down_left, "b", 0, left)
    down_right = fold(down_right, "l", 0, left)
    up_sum = scatter_step(up_sum, "h", 1, left)
    down_sum = fold_a(down_dw, rows, left)
    output_view = scatter_step(output_view, "b", 1, left)
    left = scatter_step(left, "b", 0)
    right = scatter_step(right, "l", 0)
    grad_nattn = jnp.concatenate([left, right], axis=-1)
    grad_input, _ = norm_back(own.astype(F32), attn_gain_full, grad_nattn)
    input_grad = (grad_hidden + grad_input).astype(BF)
    down_sum = scatter_step(down_sum, "h", 1)
    qkv_sum = scatter_step(fold_a(slab, rows, left), "h", 1)
    output_view = scatter_step(output_view, "l", 2)
    output_view = scatter_step(output_view, "a", 0)
    output_grad = scatter_step(output_view, "h", 0)
    down_out = jnp.concatenate([down_left, down_right], axis=-1)
    output = jnp.where(valid, hidden + down_out, 0.0).astype(BF)
    qkv_grad = fold_team(qkv_sum, rows)
    gain_grads = jnp.sum(qkv_grad[:, :, V_END : V_END + 2], axis=1)
    gate_grad, up_grad, down_grad = (
        fold_team(x, rows).reshape(rows, -1) for x in (gate_sum, up_sum, down_sum)
    )
    return (
        output[None],
        input_grad[None],
        gain_grads[:, 0],
        qkv_grad[:, :, :Q_END].reshape(rows, -1),
        qkv_grad[:, :, Q_END:K_END].reshape(rows, -1),
        qkv_grad[:, :, K_END:V_END].reshape(rows, -1),
        output_grad,
        gain_grads[:, 1],
        gate_grad,
        up_grad,
        down_grad,
    )


def solution(mesh):
    n_dp, n_seq = mesh.shape["dp"], mesh.shape["seq"]
    fine = Mesh(mesh.devices.reshape(n_dp // 4, 2, 2, n_seq // 2, 2), EVERY)
    tokens = P(("a", "b", "c"), ("h", "l"), None)
    matrix = P(EVERY, None)
    vector = P(EVERY)
    placed = (
        tokens,
        P(("a", "b", "c")),
        P(("a", "b", "c"), ("h", "l")),
        vector,
        matrix,
        matrix,
        matrix,
        matrix,
        vector,
        matrix,
        matrix,
        matrix,
        tokens,
    )
    return jax.shard_map(
        local,
        mesh=fine,
        in_specs=placed,
        out_specs=(
            tokens, tokens, vector, matrix, matrix, matrix, matrix, vector, matrix, matrix, matrix
        ),
        check_vma=False,
    )
```

```python
import functools
import math

import jax
import jax.numpy as jnp
from jax import lax
from jax.experimental import pallas as pl
from jax.experimental.pallas import tpu as pltpu
from jax.sharding import Mesh
from jax.sharding import PartitionSpec as P

HEADS = 32
GROUPS = 8
SIZE = 64
SHARE = HEADS // GROUPS
EPS = 1e-05
TEAM = ("b", "c", "l")
EVERY = ("a", "b", "c", "h", "l")
BF = jnp.bfloat16
F32 = jnp.float32


def rope_tables(positions):
    index = jnp.arange(SIZE // 2, dtype=F32)
    frequency = 1.0 / 500000.0 ** (2.0 * index / SIZE)
    wavelength = 2.0 * math.pi / frequency
    blending = (8192.0 / wavelength - 1.0) / (4.0 - 1.0)
    middle = (1.0 - blending) * frequency / 32.0 + blending * frequency
    scaled = jnp.where(
        wavelength < 8192.0 / 4.0,
        frequency,
        jnp.where(wavelength > 8192.0, frequency / 32.0, middle),
    )
    angles = positions.astype(F32)[..., None] * scaled
    angles = jnp.concatenate([angles, angles], axis=-1)
    return jnp.cos(angles), jnp.sin(angles)


def rope_lanes(cosine, sine):
    signed = jnp.where(jnp.arange(SIZE) < SIZE // 2, -sine, sine)
    ones, zeros = jnp.ones_like(cosine), jnp.zeros_like(sine)
    return (
        jnp.concatenate([cosine, cosine, cosine, ones], axis=-1),
        jnp.concatenate([signed, signed, signed, zeros], axis=-1),
    )


def swap_halves(v):
    lane = lax.broadcasted_iota(jnp.int32, v.shape, 1)
    low = lax.rem(lane, SIZE) < SIZE // 2
    return jnp.where(low, pltpu.roll(v, 128 - SIZE // 2, 1), pltpu.roll(v, SIZE // 2, 1))


def rope_blocks(v, cosine, sine, sign):
    outs = []
    for n in range(3):
        block = v[:, n * 128 : (n + 1) * 128]
        cols = slice(128, 256) if n == 2 else slice(0, 128)
        outs.append(block * cosine[:, cols] + sign * swap_halves(block) * sine[:, cols])
    return jnp.concatenate(outs, axis=-1)


def shift(value, axis, step):
    n = lax.axis_size(axis)
    return lax.ppermute(value, axis, [(i, (i + step) % n) for i in range(n)])


def after(value, earlier):
    return lax.optimization_barrier((value, earlier))[0]


def scatter_step(value, axis, dim, pin=None):
    n = lax.axis_size(axis)
    me = lax.axis_index(axis)
    kept = lax.dynamic_index_in_dim(value, me, dim, keepdims=False).astype(F32)
    for s in range(1, n):
        sent = lax.dynamic_index_in_dim(value, lax.rem(me + s, n), dim, keepdims=False)
        arrived = shift(sent.astype(BF), axis, s)
        if pin is not None:
            arrived = after(arrived, pin)
        kept = kept + arrived.astype(F32)
    return kept


def team_scatter(partial):
    width = partial.shape[-1]
    view = partial.reshape(2, 2, 2, -1, width)
    view = scatter_step(view, "c", 1)
    left = scatter_step(view[..., : width // 2], "l", 1)
    left = scatter_step(left, "b", 0)
    right = scatter_step(view[..., width // 2 :], "b", 0)
    right = scatter_step(right, "l", 0)
    return jnp.concatenate([left, right], axis=-1)


def together(*values):
    return lax.optimization_barrier(values)


def fold_a(partial, rows, pin=None):
    view = partial.reshape(lax.axis_size("a"), 4, lax.axis_size("h"), 2 * rows, partial.shape[-1])
    return scatter_step(view, "a", 0, pin)


def fold_team(view, rows):
    owned = lax.all_to_all(
        view.reshape(8, rows, view.shape[-1]).astype(BF), TEAM, 0, 0, tiled=True
    )
    return owned.transpose(1, 0, 2).astype(F32)


def fold(value, axis, dim, pin=None):
    kept = lax.index_in_dim(value, 0, dim, keepdims=False).astype(F32)
    sent = lax.index_in_dim(value, 1, dim, keepdims=False).astype(BF)
    arrived = shift(sent, axis, 1)
    if pin is not None:
        arrived = after(arrived, pin)
    return kept + arrived.astype(F32)


def dot(a, b, over):
    return lax.dot_general(a, b, ((over[0], over[1]), ((), ())), preferred_element_type=F32)


NN = ((1,), (0,))
NT = ((1,), (1,))
TN = ((0,), (0,))


def softmax_parts(late, length, q, keys, early_keys):
    rows = q.shape[0]
    slot = late * rows + lax.broadcasted_iota(jnp.int32, (rows, rows), 0)
    key_slot = late * rows + lax.broadcasted_iota(jnp.int32, (rows, rows), 1)
    allowed = (key_slot <= slot) & (key_slot < length)
    own = jnp.where(allowed, dot(q, keys, NT) * SIZE**-0.5, -1e30)
    early_slot = lax.broadcasted_iota(jnp.int32, (rows, rows), 1)
    early = jnp.where(
        (early_slot < late * rows) & (early_slot < length), dot(q, early_keys, NT) * SIZE**-0.5, -1e30
    )
    peak = jnp.maximum(
        jnp.max(own, axis=-1, keepdims=True), jnp.max(early, axis=-1, keepdims=True)
    )
    own, early = jnp.exp(own - peak), jnp.exp(early - peak)
    total = jnp.sum(own, axis=-1, keepdims=True) + jnp.sum(early, axis=-1, keepdims=True)
    part = 1.0 / total
    return own * part, early * part


Q_END, K_END, V_END = SHARE * SIZE, SHARE * SIZE + SIZE, SHARE * SIZE + 2 * SIZE


def project_kernel(x_ref, gain_ref, w_ref, cos_ref, sin_ref, normed_ref, out_ref):
    x = x_ref[0].astype(F32)
    normed = (x * norm_parts(x) * gain_ref[...]).astype(BF)
    normed_ref[...] = normed
    qkv = dot(normed, w_ref[...], NN)
    out_ref[...] = rope_blocks(qkv, cos_ref[...], sin_ref[...], 1.0).astype(BF)


def project_call(team_packed, gain, w_qkv, cosine, sine):
    _, rows, _ = team_packed.shape
    width = gain.shape[-1]
    return pl.pallas_call(
        project_kernel,
        grid=(8,),
        in_specs=[
            pl.BlockSpec((1, rows, width), lambda i: (i, 0, 0)),
            pl.BlockSpec((1, width), lambda i: (0, 0)),
            pl.BlockSpec((width, V_END), lambda i: (0, 0)),
            pl.BlockSpec((rows, 256), lambda i: (i, 0)),
            pl.BlockSpec((rows, 256), lambda i: (i, 0)),
        ],
        out_specs=[
            pl.BlockSpec((rows, width), lambda i: (i, 0)),
            pl.BlockSpec((rows, V_END), lambda i: (i, 0)),
        ],
        out_shape=[
            jax.ShapeDtypeStruct((8 * rows, width), BF),
            jax.ShapeDtypeStruct((8 * rows, V_END), BF),
        ],
        compiler_params=pltpu.CompilerParams(vmem_limit_bytes=40 * 2**20),
        cost_estimate=pl.CostEstimate(
            flops=16 * rows * width * V_END, bytes_accessed=24 * 2**20, transcendentals=0
        ),
    )(team_packed, gain, w_qkv, cosine, sine)


def unrotate_kernel(own_ref, back_ref, cos_ref, sin_ref, out_ref):
    own = own_ref[...]
    tail = own[:, Q_END:] + back_ref[...].astype(F32)
    total = jnp.concatenate([own[:, :Q_END], tail], axis=-1)
    out_ref[...] = rope_blocks(total, cos_ref[...], sin_ref[...], -1.0).astype(BF)


def unrotate_call(own, back, cosine, sine):
    tokens = own.shape[0]
    rows = tokens // 4

    def spec(x):
        return pl.BlockSpec((rows, x.shape[1]), lambda i: (i, 0))

    return pl.pallas_call(
        unrotate_kernel,
        grid=(4,),
        in_specs=[spec(x) for x in (own, back, cosine, sine)],
        out_specs=spec(own),
        out_shape=jax.ShapeDtypeStruct(own.shape, BF),
        cost_estimate=pl.CostEstimate(flops=10**7, bytes_accessed=9 * 2**20, transcendentals=0),
    )(own, back, cosine, sine)


def forward_kernel(late_ref, length_ref, qkv_ref, early_ref, o_ref):
    late, length = late_ref[0], length_ref[pl.program_id(0)]
    keys, values = qkv_ref[0, :, Q_END:K_END], qkv_ref[0, :, K_END:V_END]
    early_keys, early_values = early_ref[0, :, :SIZE], early_ref[0, :, SIZE:]
    outs = []
    for head in range(SHARE):
        q = qkv_ref[0, :, head * SIZE : (head + 1) * SIZE]
        own, early = softmax_parts(late, length, q, keys, early_keys)
        outs.append(dot(own.astype(BF), values, NN) + dot(early.astype(BF), early_values, NN))
    o_ref[0] = jnp.concatenate(outs, axis=-1).astype(BF)


def backward_kernel(late_ref, length_ref, qkv_ref, early_ref, g_ref, d_ref, ed_ref):
    late, length = late_ref[0], length_ref[pl.program_id(0)]
    keys, values = qkv_ref[0, :, Q_END:K_END], qkv_ref[0, :, K_END:V_END]
    early_keys, early_values = early_ref[0, :, :SIZE], early_ref[0, :, SIZE:]
    scale = SIZE**-0.5
    dqs = []
    dk = dv = edk = edv = 0.0
    for head in range(SHARE):
        q = qkv_ref[0, :, head * SIZE : (head + 1) * SIZE]
        g = g_ref[0, :, head * SIZE : (head + 1) * SIZE]
        own, early = softmax_parts(late, length, q, keys, early_keys)
        dp, edp = dot(g, values, NT), dot(g, early_values, NT)
        inner = jnp.sum(own * dp, axis=-1, keepdims=True) + jnp.sum(
            early * edp, axis=-1, keepdims=True
        )
        ds = (own * (dp - inner)).astype(BF)
        eds = (early * (edp - inner)).astype(BF)
        dqs.append((dot(ds, keys, NN) + dot(eds, early_keys, NN)) * scale)
        dv = dv + dot(own.astype(BF), g, TN)
        edv = edv + dot(early.astype(BF), g, TN)
        dk = dk + dot(ds, q, TN)
        edk = edk + dot(eds, q, TN)
    d_ref[0] = jnp.concatenate(dqs + [dk * scale, dv], axis=-1)
    ed_ref[0] = jnp.concatenate([edk * scale, edv], axis=-1).astype(BF)


def attention_call(kernel, late, lengths, arrays, outs, flops):
    count, rows, _ = arrays[0].shape

    def spec(width):
        return pl.BlockSpec((1, rows, width), lambda s, *_: (s, 0, 0))

    return pl.pallas_call(
        kernel,
        grid_spec=pltpu.PrefetchScalarGridSpec(
            num_scalar_prefetch=2,
            grid=(count,),
            in_specs=[spec(x.shape[-1]) for x in arrays],
            out_specs=[spec(width) for width, _ in outs],
        ),
        out_shape=[jax.ShapeDtypeStruct((count, rows, width), kind) for width, kind in outs],
        compiler_params=pltpu.CompilerParams(vmem_limit_bytes=48 * 2**20),
        cost_estimate=pl.CostEstimate(flops=flops, bytes_accessed=8 * 2**20, transcendentals=2**23),
    )(late, lengths, *arrays)


MESH = pl.DeviceIdType.MESH


def ffn_kernel(
    own_ref,
    grad_ref,
    *refs,
):
    n_pieces = len(refs) - 28
    ffn_body(own_ref, grad_ref, refs[:n_pieces], *refs[n_pieces:])


def ffn_body(
    own_ref,
    grad_ref,
    piece_refs,
    gn_ref,
    dn_ref,
    dwg_ref,
    dwu_ref,
    dwd_ref,
    wg,
    wu,
    wd,
    xs,
    gs,
    act,
    gg,
    gu,
    send_sib,
    recv_sib,
    send_own,
    recv_own,
    stage,
    local_sem,
    grad_sem,
    ag_send,
    ag_recv,
    sib_send,
    sib_recv,
    own_send,
    own_recv,
    stage_sem,
    credit,
):
    b, c, l = lax.axis_index("b"), lax.axis_index("c"), lax.axis_index("l")
    rows, width = own_ref.shape
    tile = wg.shape[1]
    sibling = {"c": 1 - c}

    def chip(k):
        return {"b": lax.rem(b + lax.rem(k, 2), 2), "l": lax.rem(l + k // 2, 2)}

    barrier = pltpu.get_barrier_semaphore()
    for peer in (sibling, chip(1), chip(2), chip(3)):
        pl.semaphore_signal(barrier, inc=1, device_id=peer, device_id_type=MESH)
    pl.semaphore_wait(barrier, 4)

    def part(slot):
        return pl.ds(pl.multiple_of(slot * rows, rows), rows)

    def gather_copy(source, slot, peer):
        return pltpu.make_async_remote_copy(
            src_ref=source,
            dst_ref=xs.at[part(slot)],
            send_sem=ag_send.at[slot],
            recv_sem=ag_recv.at[slot],
            device_id=peer,
            device_id_type=MESH,
        )

    def forward_copy(k):
        return gather_copy(xs.at[part(2 * k)], 2 * k + 1, sibling)

    def diagonal(half):
        slot, peer, sem = ((2, chip(2), 6), (4, chip(1), 0))[half]
        shift_rows = half * (rows // 2)
        return pltpu.make_async_remote_copy(
            src_ref=xs.at[pl.ds(slot * rows + shift_rows, rows // 2)],
            dst_ref=xs.at[pl.ds(6 * rows + shift_rows, rows // 2)],
            send_sem=ag_send.at[sem],
            recv_sem=ag_recv.at[sem],
            device_id=peer,
            device_id_type=MESH,
        )

    def sibling_copy(k):
        spot = lax.rem(k, 2)
        return pltpu.make_async_remote_copy(
            src_ref=send_sib.at[spot],
            dst_ref=recv_sib.at[spot],
            send_sem=sib_send.at[spot],
            recv_sem=sib_recv.at[spot],
            device_id=sibling,
            device_id_type=MESH,
        )

    def owner_copy(k):
        return pltpu.make_async_remote_copy(
            src_ref=send_own.at[k - 1],
            dst_ref=recv_own.at[k - 1],
            send_sem=own_send.at[k - 1],
            recv_sem=own_recv.at[k - 1],
            device_id=chip(k),
            device_id_type=MESH,
        )

    def grad_copy(slot):
        k, dc = slot // 2, lax.rem(slot, 2)
        db, dl = lax.rem(k, 2), k // 2
        source = (lax.rem(b + db, 2) * 2 + lax.rem(c + dc, 2)) * 2 + lax.rem(l + dl, 2)
        return pltpu.make_async_copy(grad_ref.at[source], gs.at[part(slot)], grad_sem.at[slot])

    def down_copy(spot, slot):
        cols = pl.ds(spot * tile, tile)
        return pltpu.make_async_copy(stage.at[spot], dn_ref.at[slot, :, cols], stage_sem.at[spot])

    gather_copy(own_ref, 1, sibling).start()
    for k in (1, 2):
        gather_copy(own_ref, 2 * k, chip(k)).start()
    own_copy = pltpu.make_async_copy(own_ref, xs.at[part(0)], local_sem.at[0])
    own_copy.start()
    a, h = lax.axis_index("a"), lax.axis_index("h")
    n_a, n_h = lax.axis_size("a"), lax.axis_size("h")
    chunk = piece_refs[0].shape[1]
    for j, target in enumerate((wg, wu, wd)):
        near, near_a, far, far_a = piece_refs[4 * j : 4 * j + 4]
        for dh, first, rest in ((0, near, near_a), (1, far, far_a)):
            for da in range(n_a):
                source = rest.at[da - 1] if da else first
                ra, rh = lax.rem(a + n_a - da, n_a), lax.rem(h + dh, n_h)
                for pair in range(4):
                    start = pl.multiple_of(((ra * 4 + pair) * n_h + rh) * chunk, chunk)
                    pltpu.make_async_copy(
                        source.at[pair], target.at[pl.ds(start, chunk)], local_sem.at[1 + j]
                    ).start()
    for slot in range(8):
        grad_copy(slot).start()
    for j, target in enumerate((wg, wu, wd)):
        pltpu.make_async_copy(target, target, local_sem.at[1 + j]).wait()
    own_copy.wait()

    def block(i, carry):
        k, second = i // 2, lax.rem(i, 2)
        slot = 2 * k + 1 - second
        spot = lax.rem(k, 2)
        for at, ready in ((2, 1), (3, 2), (5, 3)):

            @pl.when(i == at)
            def _():
                if ready < 3:
                    gather_copy(own_ref, 2 * ready, chip(ready)).wait_recv()
                    diagonal(ready - 1).start()
                else:
                    diagonal(0).wait_recv()
                    diagonal(1).wait_recv()
                forward_copy(ready).start()

        @pl.when(second == 0)
        def _():
            gather_copy(own_ref, slot, sibling).wait_recv()

        grad_copy(slot).wait()
        for piece in (slice(0, tile // 2), slice(tile // 2, tile)):
            gate = dot(xs[part(slot), :], wg[:, piece], NN)
            up = dot(xs[part(slot), :], wu[:, piece], NN)
            grad_act = dot(gs[part(slot), :], wd[:, piece], NN)
            sigmoid = jax.nn.sigmoid(gate)
            silu = gate * sigmoid
            act[part(slot), piece] = (silu * up).astype(BF)
            gu[part(slot), piece] = (grad_act * silu).astype(BF)
            slope = sigmoid * (1.0 + gate * (1.0 - sigmoid))
            gg[part(slot), piece] = (grad_act * up * slope).astype(BF)

        @pl.when((second == 0) & (k >= 2))
        def _():
            sibling_copy(k).wait_send()

        @pl.when(second == 1)
        def _():
            sibling_copy(k).wait_recv()

        for start in range(0, width, tile):
            cols = slice(start, start + tile)
            part_gn = dot(gg[part(slot), :], wg[cols, :], NT)
            part_gn += dot(gu[part(slot), :], wu[cols, :], NT)

            @pl.when(second == 0)
            def _():
                send_sib[spot, :, cols] = part_gn.astype(BF)

            @pl.when(i == 1)
            def _():
                gn_ref[:, cols] = part_gn + recv_sib[spot, :, cols].astype(F32)

            @pl.when((second == 1) & (k > 0))
            def _():
                send_own[k - 1, :, cols] = (part_gn + recv_sib[spot, :, cols].astype(F32)).astype(BF)

        @pl.when((second == 0) & (k >= 2))
        def _():
            pl.semaphore_wait(credit, 1)

        @pl.when(second == 0)
        def _():
            sibling_copy(k).start()

        @pl.when((second == 1) & (k < 2))
        def _():
            pl.semaphore_signal(credit, inc=1, device_id=sibling, device_id_type=MESH)

        @pl.when((second == 1) & (k > 0))
        def _():
            owner_copy(k).start()

        for at in range(width // tile):
            part_dn = dot(act[part(slot), :], wd[at * tile : (at + 1) * tile, :], NT)

            @pl.when(i >= 1)
            def _():
                down_copy(at, slot).wait()

            stage[at] = part_dn.astype(BF)
            down_copy(at, slot).start()
        return carry

    lax.fori_loop(0, 8, block, 0)
    for at in range(width // tile):
        down_copy(at, 0).wait()

    step = rows

    def weight_copy(j, which, target):
        return pltpu.make_async_copy(
            stage.at[which],
            target.at[pl.ds(pl.multiple_of(j * step, step), step)],
            stage_sem.at[which],
        )

    def weights(j, carry):
        cols = pl.ds(pl.multiple_of(j * step, step), step)
        for which, (left, right, target) in enumerate(
            ((xs, gg, dwg_ref), (xs, gu, dwu_ref), (gs, act, dwd_ref))
        ):

            @pl.when(j > 0)
            def _():
                weight_copy(j, which, target).wait()

            stage[which] = dot(left[:, cols], right[...], TN).astype(BF)
            weight_copy(j, which, target).start()
        return carry

    lax.fori_loop(0, width // step, weights, 0)

    for k in (1, 2, 3):
        owner_copy(k).wait_recv()
        gn_ref[...] += recv_own[k - 1].astype(F32)
    for which, target in enumerate((dwg_ref, dwu_ref, dwd_ref)):
        weight_copy(0, which, target).wait()
    for k in (0, 1):
        sibling_copy(k).wait_send()
    gather_copy(own_ref, 1, sibling).wait_send()
    for k in (1, 2):
        gather_copy(own_ref, 2 * k, chip(k)).wait_send()
        diagonal(k - 1).wait_send()
    for k in (1, 2, 3):
        forward_copy(k).wait_send()
        owner_copy(k).wait_send()


def ffn_call(own, team_grad, pieces):
    rows, width = own.shape
    hidden = pieces[0].shape[-1]
    team = 8 * rows
    anywhere = pl.BlockSpec(memory_space=pl.ANY)
    stages = max(3, width // hidden)
    return pl.pallas_call(
        ffn_kernel,
        in_specs=[anywhere] * (2 + len(pieces)),
        out_specs=[pl.BlockSpec(memory_space=pltpu.VMEM)] + [anywhere] * 4,
        out_shape=[
            jax.ShapeDtypeStruct((rows, width), F32),
            jax.ShapeDtypeStruct((8, rows, width), BF),
        ]
        + [jax.ShapeDtypeStruct((width, hidden), BF)] * 3,
        scratch_shapes=[pltpu.VMEM((width, hidden), BF)] * 3
        + [pltpu.VMEM((team, width), BF)] * 2
        + [pltpu.VMEM((team, hidden), BF)] * 3
        + [pltpu.VMEM((2, rows, width), BF)] * 2
        + [pltpu.VMEM((3, rows, width), BF)] * 2
        + [pltpu.VMEM((stages, rows, hidden), BF)]
        + [pltpu.SemaphoreType.DMA((n,)) for n in (4, 8, 8, 8, 2, 2, 3, 3, stages)]
        + [pltpu.SemaphoreType.REGULAR],
        compiler_params=pltpu.CompilerParams(
            collective_id=0, has_side_effects=True, vmem_limit_bytes=60 * 2**20
        ),
        cost_estimate=pl.CostEstimate(
            flops=18 * team * width * hidden, bytes_accessed=60 * 2**20, transcendentals=team * hidden
        ),
    )(own, team_grad, *pieces)


def opening_kernel(
    tok_ref,
    grad_ref,
    qkv_ref,
    gain_ref,
    gate_ref,
    up_ref,
    down_ref,
    toks,
    grads,
    slab,
    gains,
    gate0,
    gate_h,
    gate_a,
    gate_far,
    up0,
    up_h,
    up_a,
    down0,
    down_a,
    team_send,
    team_recv,
    tok_send,
    tok_recv,
    local_sem,
    h_send,
    h_recv,
    a_send,
    a_recv,
):
    a, b, c, h, l = (lax.axis_index(axis) for axis in EVERY)
    n_a = lax.axis_size("a")
    n_rows = qkv_ref.shape[0]
    q_wide, f_wide, g_rows = slab.shape[-1], gate0.shape[-1], gain_ref.shape[0]

    def flip(off):
        return lax.rem(b + off // 4, 2), lax.rem(c + off // 2 % 2, 2), lax.rem(l + off % 2, 2)

    def peer(off):
        pb, pc, p_l = flip(off)
        return {"b": pb, "c": pc, "l": p_l}

    def number(off):
        pb, pc, p_l = flip(off)
        return (pb * 2 + pc) * 2 + p_l

    def a_peer(step):
        return {"a": lax.rem(a + step, n_a)}

    h_peer = {"h": 1 - h}
    barrier = pltpu.get_barrier_semaphore()
    others = [peer(off) for off in range(1, 8)] + [h_peer] + [a_peer(s) for s in range(1, n_a)]
    for other in others:
        pl.semaphore_signal(barrier, inc=1, device_id=other, device_id_type=MESH)
    pl.semaphore_wait(barrier, len(others))

    def source(which, off):
        t = number(off)
        if which == 0:
            return qkv_ref.at[:, pl.ds(pl.multiple_of(t * q_wide, 128), q_wide)]
        if which == 1:
            return gain_ref
        ref = (gate_ref, up_ref, down_ref)[which - 2]
        return ref.at[:, pl.ds(pl.multiple_of(t * f_wide, 128), f_wide)]

    def place(which, off):
        pb, pc, p_l = flip(off)
        pair = pb * 2 + pc
        rows = pl.ds(pl.multiple_of(p_l * n_rows, n_rows), n_rows)
        if which == 0:
            return slab.at[a, pair, h, rows]
        if which == 1:
            return gains.at[a, pair, h, pl.ds(pl.multiple_of(p_l * g_rows, g_rows), g_rows)]
        return (gate0, up0, down0)[which - 2].at[pair, rows]

    def team_copy(which, off, arriving=False):
        return pltpu.make_async_remote_copy(
            src_ref=source(which, off),
            dst_ref=place(which, off if arriving else 0),
            send_sem=team_send.at[which, off],
            recv_sem=team_recv.at[which, off],
            device_id=peer(off),
            device_id_type=MESH,
        )

    def own_copy(which):
        return pltpu.make_async_copy(source(which, 0), place(which, 0), local_sem.at[which])

    def tok_copy(which, from_off, to_off, sem):
        whole = (toks, grads)[which]
        held = (tok_ref, grad_ref)[which] if sem < 6 and sem != 3 else whole.at[number(from_off)]
        return pltpu.make_async_remote_copy(
            src_ref=held,
            dst_ref=whole.at[number(from_off)],
            send_sem=tok_send.at[which, sem],
            recv_sem=tok_recv.at[which, sem],
            device_id=peer(to_off),
            device_id_type=MESH,
        )

    def forward(which, off):
        return tok_copy(which, off, 2, off + 2)

    def diagonal(which, half, arriving=False):
        whole = (toks, grads)[which]
        rows = whole.shape[1] // 2
        owner, to, sem = ((4, 1, 5), (1, 4, 0))[half]
        spot = pl.ds(half * rows, rows)
        return pltpu.make_async_remote_copy(
            src_ref=whole.at[number(owner), spot],
            dst_ref=whole.at[number(5 if arriving else owner), spot],
            send_sem=tok_send.at[which, sem],
            recv_sem=tok_recv.at[which, sem],
            device_id=peer(to),
            device_id_type=MESH,
        )

    def hand_on(which):
        for half, off in enumerate((4, 1)):
            tok_copy(which, off, off, off).wait_recv()
            diagonal(which, half).start()
            forward(which, off).start()

    def diagonal_arrived(which):
        for half in (0, 1):
            diagonal(which, half, arriving=True).wait_recv()
        forward(which, 5).start()

    def region(which, ra, rh):
        if which == 0:
            return slab.at[ra, :, rh]
        return gains.at[ra, :, rh]

    def h_copy(which, arriving=False):
        if which >= 2:
            src, dst = ((gate0, gate_h), (up0, up_h))[which - 2]
        else:
            src = region(which, a, h)
            dst = region(which, a, 1 - h if arriving else h)
        return pltpu.make_async_remote_copy(
            src_ref=src,
            dst_ref=dst,
            send_sem=h_send.at[which],
            recv_sem=h_recv.at[which],
            device_id=h_peer,
            device_id_type=MESH,
        )

    def a_copy(which, step, arriving=False):
        if which >= 4:
            src = (gate0, up0, down0, gate_h)[which - 4]
            dst = (gate_a, up_a, down_a, gate_far)[which - 4].at[step - 1]
        else:
            rh = h if which < 2 else 1 - h
            src = region(which % 2, a, rh)
            dst = region(which % 2, lax.rem(a + n_a - step, n_a) if arriving else a, rh)
        return pltpu.make_async_remote_copy(
            src_ref=src,
            dst_ref=dst,
            send_sem=a_send.at[which, step - 1],
            recv_sem=a_recv.at[which, step - 1],
            device_id=a_peer(step),
            device_id_type=MESH,
        )

    def team_arrived(which):
        own_copy(which).wait()
        for off in range(1, 8):
            team_copy(which, off, arriving=True).wait_recv()

    away = (4, 1, 5)
    steps = range(1, n_a)

    def team_start(*which):
        for w in which:
            for off in range(1, 8):
                team_copy(w, off).start()
            own_copy(w).start()

    def a_start(*which):
        for w in which:
            for step in steps:
                a_copy(w, step).start()

    team_start(0, 1)
    own_toks = [
        pltpu.make_async_copy(src, dst.at[number(0)], local_sem.at[5 + n])
        for n, (src, dst) in enumerate(((tok_ref, toks), (grad_ref, grads)))
    ]
    for which in (0, 1):
        own_toks[which].start()
        tok_copy(which, 0, 2, 2).start()
    team_arrived(0)
    team_arrived(1)
    h_copy(0).start()
    h_copy(1).start()
    a_start(0, 1)
    team_start(2, 3)
    team_arrived(2)
    a_start(4)
    for off in (4, 1):
        tok_copy(0, 0, off, off).start()
    team_arrived(3)
    a_start(5)
    team_start(4)
    for which in (0, 1):
        h_copy(which, arriving=True).wait_recv()
    h_copy(2).start()
    a_start(2, 3)
    hand_on(0)
    for off in (4, 1):
        tok_copy(1, 0, off, off).start()
    diagonal_arrived(0)
    team_arrived(4)
    a_start(6)
    h_copy(2).wait_recv()
    h_copy(3).start()
    a_start(7)
    hand_on(1)
    diagonal_arrived(1)
    for which in (0, 1):
        own_toks[which].wait()
        tok_copy(which, 2, 2, 2).wait_recv()
        for off in away:
            tok_copy(which, off + 2, 2, off + 2).wait_recv()
    for which in range(8):
        for step in steps:
            a_copy(which, step, arriving=True).wait_recv()
            a_copy(which, step).wait_send()
    h_copy(3).wait_recv()
    for which in range(4):
        h_copy(which).wait_send()
    for which in range(5):
        for off in range(1, 8):
            team_copy(which, off).wait_send()
    for which in (0, 1):
        for off in (2, 4, 1):
            tok_copy(which, 0, off, off).wait_send()
        for half in (0, 1):
            diagonal(which, half).wait_send()
        for off in away:
            forward(which, off).wait_send()


def opening_call(packed, grad_out, qkv_local, gain_tile, gate, up, down):
    n_a, n_h = lax.axis_size("a"), lax.axis_size("h")
    rows = gate.shape[0]
    q_wide, f_wide = qkv_local.shape[1] // 8, gate.shape[1] // 8
    anywhere = pl.BlockSpec(memory_space=pl.ANY)
    piece = (4, 2 * rows, f_wide)
    shapes = [
        (8,) + packed.shape,
        (8,) + grad_out.shape,
        (n_a, 4, n_h, 2 * rows, q_wide),
        (n_a, 4, n_h, 2 * gain_tile.shape[0], 128),
        piece,
        piece,
        (n_a - 1,) + piece,
        (n_a - 1,) + piece,
        piece,
        piece,
        (n_a - 1,) + piece,
        piece,
        (n_a - 1,) + piece,
    ]
    dma = pltpu.SemaphoreType.DMA
    return pl.pallas_call(
        opening_kernel,
        in_specs=[anywhere] * 7,
        out_specs=[anywhere] * 13,
        out_shape=[jax.ShapeDtypeStruct(shape, BF) for shape in shapes],
        scratch_shapes=[
            dma((5, 8)),
            dma((5, 8)),
            dma((2, 8)),
            dma((2, 8)),
            dma((7,)),
            dma((4,)),
            dma((4,)),
            dma((8, n_a - 1)),
            dma((8, n_a - 1)),
        ],
        compiler_params=pltpu.CompilerParams(
            collective_id=1, has_side_effects=True, vmem_limit_bytes=8 * 2**20
        ),
        cost_estimate=pl.CostEstimate(flops=0, bytes_accessed=300 * 2**20, transcendentals=0),
    )(packed, grad_out, qkv_local, gain_tile, gate, up, down)


def norm_parts(value):
    return lax.rsqrt(jnp.mean(value * value, axis=-1, keepdims=True) + EPS)


def norm_back(value, gain, grad):
    r = norm_parts(value)
    hat = value * r
    scaled = grad * gain
    return r * (scaled - hat * jnp.mean(scaled * hat, axis=-1, keepdims=True)), hat


def local(
    inputs,
    lengths,
    positions,
    attn_gain,
    w_query,
    w_key,
    w_value,
    w_output,
    ffn_gain,
    w_gate,
    w_up,
    w_down,
    out_grad,
):
    _, slots, width = inputs.shape
    rows = w_gate.shape[0]
    h, l = lax.axis_index("h"), lax.axis_index("l")
    half = 2 * slots
    q_width = SHARE * SIZE
    own_slot = (h * 2 + l) * slots + jnp.arange(slots, dtype=jnp.int32)
    valid = (own_slot < lengths[0])[:, None]
    own = inputs[0]
    grad_out = jnp.where(valid, out_grad[0], jnp.zeros((), BF))

    numbers = jnp.stack([positions[0], jnp.broadcast_to(lengths, (slots,))], axis=-1)
    digits = jnp.concatenate([numbers // 128, numbers % 128], axis=-1).astype(BF)
    packed = jnp.concatenate([own, jnp.pad(digits, ((0, 0), (0, 124)))], axis=-1)
    gain_tile = jnp.pad(jnp.stack([attn_gain, ffn_gain]), ((0, 0), (0, 64 - rows)))
    gain_tile = jnp.broadcast_to(gain_tile.reshape(1, 128), (16, 128))
    qkv_local = jnp.concatenate(
        [w.reshape(rows, 8, -1) for w in (w_query, w_key, w_value)], axis=-1
    ).reshape(rows, -1)
    (
        team_packed,
        team_grad,
        slab,
        gains,
        gate0,
        gate_h,
        gate_a,
        gate_far,
        up0,
        up_h,
        up_a,
        down0,
        down_a,
    ) = opening_call(packed, grad_out, qkv_local, gain_tile, w_gate, w_up, w_down)
    slab, w_output = together(slab, w_output)
    w_out = lax.all_gather(w_output, EVERY, axis=0, tiled=True)
    steps = range(1, lax.axis_size("a"))
    w_qkv = slab.reshape(width, V_END)
    gains = gains.reshape(-1, 16, 128)[:, 0].astype(F32)
    attn_gain_full = gains[:, :rows].reshape(1, width)
    ffn_gain_full = gains[:, 64 : 64 + rows].reshape(1, width)
    down_h = shift(down0, "h", 1)
    up_far = [shift(up_h, "a", s) for s in steps]

    tokens = 8 * slots
    digits = team_packed[:, :, width : width + 4].reshape(tokens, 4).astype(jnp.int32)
    cosine, sine = rope_lanes(*rope_tables(digits[:, 0] * 128 + digits[:, 2]))
    team_lengths = (digits[:, 1] * 128 + digits[:, 3])[::half]
    normed_attn, qkv = project_call(team_packed, attn_gain_full, w_qkv, cosine, sine)
    qkv = qkv.reshape(4, half, V_END)
    early = lax.ppermute(qkv[:, :, Q_END:], "h", [(0, 1)])
    late = h.astype(jnp.int32).reshape(1)
    attended = attention_call(
        forward_kernel, late, team_lengths, (qkv, early), [(q_width, BF)], 3 * 10**9
    )[0]
    attended, down_h = together(attended, down_h)
    down_far = [shift(down_h, "a", s) for s in steps]
    attended = lax.all_to_all(attended.reshape(8, slots, q_width), TEAM, 0, 0, tiled=True)
    attended = attended.transpose(1, 0, 2).reshape(slots, HEADS * SIZE)

    hidden = own.astype(F32) + dot(attended, w_out, NN)
    normed_ffn = (hidden * norm_parts(hidden) * ffn_gain_full).astype(BF)

    pieces = [gate0, gate_a, gate_h, gate_far]
    pieces += [up0, up_a, up_h, jnp.stack(up_far)]
    pieces += [down0, down_a, down_h, jnp.stack(down_far)]
    grad_nffn, down_part, gate_dw, up_dw, down_dw = ffn_call(normed_ffn, team_grad, pieces)
    down_view = down_part.reshape(2, 2, 2, slots, width)

    grad_hidden, hat = norm_back(hidden, ffn_gain_full, grad_nffn)
    grad_hidden = grad_hidden + grad_out.astype(F32)
    ffn_gain_term = jnp.sum(grad_nffn * hat, axis=0)

    grad_branch = grad_hidden.astype(BF)
    grad_attended = dot(grad_branch, w_out, NT).astype(BF)
    grad_heads = lax.all_to_all(
        grad_attended.reshape(slots, 8, q_width).transpose(1, 0, 2), TEAM, 0, 0, tiled=True
    ).reshape(4, half, q_width)
    down_view = fold(down_view, "c", 2)
    output_part = dot(attended, grad_branch, TN).astype(BF)
    grad_heads, down_view, output_part = together(grad_heads, down_view, output_part)
    grad_own, grad_early = attention_call(
        backward_kernel,
        late,
        team_lengths,
        (qkv, early, grad_heads),
        [(V_END, F32), (2 * SIZE, BF)],
        8 * 10**9,
    )
    down_left = fold(down_view[..., : width // 2], "l", 0, grad_own)
    down_right = fold(down_view[..., width // 2 :], "b", 1, grad_own)
    gate_sum = fold_a(gate_dw, rows, grad_own)
    back = lax.ppermute(grad_early, "h", [(1, 0)])
    grad_qkv = unrotate_call(
        grad_own.reshape(tokens, V_END), back.reshape(tokens, 2 * SIZE), cosine, sine
    )
    n_a, n_h = lax.axis_size("a"), lax.axis_size("h")
    output_view = output_part.reshape(n_a, 2, 2, n_h, 2, rows, -1)
    output_view = scatter_step(output_view, "c", 2, grad_own)
    gate_sum = scatter_step(after(gate_sum, back), "h", 1, grad_qkv)
    up_sum = fold_a(up_dw, rows, grad_qkv)
    partial = dot(grad_qkv, w_qkv, NT)
    partial_view = scatter_step(partial.reshape(2, 2, 2, slots, width), "c", 1)
    attn_gain_term = jnp.sum(partial * normed_attn.astype(F32), axis=0) / attn_gain_full[0]
    terms = jnp.pad(jnp.stack([attn_gain_term, ffn_gain_term]), ((0, 6), (0, 0)))
    extra = lax.dot_general(
        terms, jnp.eye(8, 128, dtype=F32), ((TN[0], TN[1]), ((), ())), precision=lax.Precision.HIGHEST
    )
    slab = jnp.concatenate([dot(normed_attn, grad_qkv, TN), extra], axis=-1).astype(BF)
    slab, partial_view, up_sum = together(slab, partial_view, up_sum)
    left = scatter_step(partial_view[..., : width // 2], "l", 1, slab)
    right = scatter_step(partial_view[..., width // 2 :], "b", 0, slab)
    down_left = fold(down_left, "b", 0, left)
    down_right = fold(down_right, "l", 0, left)
    up_sum = scatter_step(up_sum, "h", 1, left)
    down_sum = fold_a(down_dw, rows, left)
    output_view = scatter_step(output_view, "b", 1, left)
    left = scatter_step(left, "b", 0)
    right = scatter_step(right, "l", 0)
    grad_nattn = jnp.concatenate([left, right], axis=-1)
    grad_input, _ = norm_back(own.astype(F32), attn_gain_full, grad_nattn)
    input_grad = (grad_hidden + grad_input).astype(BF)
    down_sum = scatter_step(down_sum, "h", 1)
    qkv_sum = scatter_step(fold_a(slab, rows, left), "h", 1)
    output_view = scatter_step(output_view, "l", 2)
    output_view = scatter_step(output_view, "a", 0)
    output_grad = scatter_step(output_view, "h", 0)
    down_out = jnp.concatenate([down_left, down_right], axis=-1)
    output = jnp.where(valid, hidden + down_out, 0.0).astype(BF)
    qkv_grad = fold_team(qkv_sum, rows)
    gain_grads = jnp.sum(qkv_grad[:, :, V_END : V_END + 2], axis=1)
    gate_grad, up_grad, down_grad = (
        fold_team(x, rows).reshape(rows, -1) for x in (gate_sum, up_sum, down_sum)
    )
    return (
        output[None],
        input_grad[None],
        gain_grads[:, 0],
        qkv_grad[:, :, :Q_END].reshape(rows, -1),
        qkv_grad[:, :, Q_END:K_END].reshape(rows, -1),
        qkv_grad[:, :, K_END:V_END].reshape(rows, -1),
        output_grad,
        gain_grads[:, 1],
        gate_grad,
        up_grad,
        down_grad,
    )


def solution(mesh):
    n_dp, n_seq = mesh.shape["dp"], mesh.shape["seq"]
    fine = Mesh(mesh.devices.reshape(n_dp // 4, 2, 2, n_seq // 2, 2), EVERY)
    tokens = P(("a", "b", "c"), ("h", "l"), None)
    matrix = P(EVERY, None)
    vector = P(EVERY)
    placed = (
        tokens,
        P(("a", "b", "c")),
        P(("a", "b", "c"), ("h", "l")),
        vector,
        matrix,
        matrix,
        matrix,
        matrix,
        vector,
        matrix,
        matrix,
        matrix,
        tokens,
    )
    return jax.shard_map(
        local,
        mesh=fine,
        in_specs=placed,
        out_specs=(
            tokens, tokens, vector, matrix, matrix, matrix, matrix, vector, matrix, matrix, matrix
        ),
        check_vma=False,
    )
```
